32 devices in a mesh: comp: 2 (over x), gx: 8 (over z, core), gy: 2 (over y).
Axes of the slice: x: 2, y: 2, z: 4, core: 2. Of those that a mesh axis runs over, the one named last changes fastest.
Arguments:
- state: float32 [2, 2, 64, 128, 256], P('comp', None, None, 'gx', 'gy'), may hold values from -6 to 6
- diffusion: float32 [2, 128, 256], P('comp', 'gx', 'gy'), may hold values from 0.03 to 0.15
- vertical: float32 [2, 64], P('comp'), may hold values from 0.01 to 0.1
- coupling: float32 [2, 128, 256], P('comp', 'gx', 'gy'), may hold values from 0.02 to 0.2
- land_sea: int32 [2, 128, 256], P('comp', 'gx', 'gy'), may hold values 0 or 1
- route_tile: int32 [2, 16, 64, 1], P('comp', ('gx', 'gy')), may hold values from 0 to 15; in each aligned block of 64 rows (0 to 63, 64 to 127, ..., all dimensions but the last counted through in order) at most 8 rows name the same one
- route_src: int32 [2, 16, 64], P('comp', ('gx', 'gy')), may hold values from 0 to 15
- route_dst: int32 [2, 16, 64], P('comp', ('gx', 'gy')), may hold values from 0 to 15
- pair_cols: int32 [2, 16, 64], P('comp', ('gx', 'gy')), may hold values from 64 to 128
- intersection: bfloat16 [2, 16, 64, 128, 128], P('comp', ('gx', 'gy')), may hold values from 0 to 0.03125
Outputs:
- final_state: float32 [2, 2, 64, 128, 256], P('comp', None, None, 'gx', 'gy')
The draws below stay inside these ranges and needn't reach their ends.
Inputs may be any that keep to these rules, and one draw needn't show every extreme that they name: `route_tile`: within the 64 pairs of one component's tile no destination tile is named more than 8 times.
All inputs are finite; a program needn't handle non-finite values. No bound on the sum of `land_sea` on one device may be relied on, other than what follows from the above.
Results may differ from the reference program's by a relative error of at most 0.0003.
Values sent between devices are 32-bit elements; how exact they have to be, the bound alone decides.
A program may use at most 128 MiB of HBM per device.

```python
import math
import jax
import jax.numpy as jnp
import numpy as np
from jax import lax

LEV = 64
KF = 2
BLK = 128
CX = 16
CY = 128
SUBSTEPS = 3
INTERVALS = 2
NX = 128
NY = 256
NT = 16
NB = 16
P_SIZE = 64
SLOTS = 8
N_GX = 8
N_GY = 2


def set_ends(array, key, smallest, high):
    place = [jax.random.randint(jax.random.fold_in(key, axis), (), 0, length) for axis, length in enumerate(array.shape)]
    longest = array.shape.index(max(array.shape))
    neighbour = place[:longest] + [(place[longest] + 1) % array.shape[longest]] + place[longest + 1:]
    return array.at[tuple(place)].set(smallest).at[tuple(neighbour)].set(high)


def shard_levels(key, extent, cuts, smallest, high):
    def one(dim, parts):
        draws = jax.random.uniform(jax.random.fold_in(jax.random.fold_in(key, 6), dim), (parts,), jnp.float32, smallest / len(cuts), high / len(cuts))
        return jnp.repeat(jnp.exp(draws), extent[dim] // parts).reshape((-1,) + (1,) * (len(extent) - dim - 1))

    gain = one(*cuts[0])
    for cut in cuts[1:]:
        gain = gain * one(*cut)
    return gain


def deal_out(key, own, number, rows, count, top, most, slope):
    ranking = jax.random.permutation(key, count)
    crowded, ordinary = shares(count, rows * top, most, slope, True), shares(count, rows * top, most, slope, False)
    places = jnp.arange(count)

    def named(sizes, rotation):
        used = int((sizes > 0).sum())
        fixed = max(1, used // 4)
        moved = fixed + (places - fixed + rotation * (used - fixed)) % max(1, count - fixed)
        return jnp.zeros((count,), jnp.int32).at[ranking[jnp.where(places < fixed, places, moved)]].set(jnp.asarray(sizes, jnp.int32))

    sizes = jnp.where(number % 4 == 0, named(crowded, number // 4), named(ordinary, number - number // 4 - 1))
    mixed = jax.random.permutation(jax.random.fold_in(own, 3), count)
    giver, taker = mixed[0:count // 2 * 2:2], mixed[1:count // 2 * 2:2]
    margin = jnp.minimum(sizes[giver] - 1, most - sizes[taker]) // 2
    margin = jnp.where((giver == ranking[0]) | (taker == ranking[0]) | (sizes[taker] == 0), 0, jnp.maximum(margin, 0))
    moved = jax.random.randint(jax.random.fold_in(own, 4), (count // 2,), 0, 1 << 20) % (margin + 1)
    sizes = sizes.at[giver].add(-moved).at[taker].add(moved)
    items = jnp.searchsorted(jnp.cumsum(sizes), jnp.arange(rows * top), side="right").astype(jnp.int32)
    listing = items.reshape(top, rows).T
    listing = listing[jax.random.permutation(jax.random.fold_in(own, 1), rows)]
    rotation = jax.random.randint(jax.random.fold_in(own, 2), (rows, 1), 0, top)
    return jnp.take_along_axis(listing, (jnp.arange(top)[None, :] + rotation) % top, axis=1)


def shares(amount, total, limit, skew, full):
    weights = [(1 << 20) // math.isqrt(grade ** skew) + 1 for grade in range(1, amount + 1)]
    largest = limit if full else min(limit, max(-(-total // amount), total * weights[0] // sum(weights)))
    least = 1 if total - largest >= amount - 1 else 0
    counts, spare = [largest] + [least] * (amount - 1), total - largest - least * (amount - 1)
    while spare > 0:
        free = [i for i in range(1, amount) if counts[i] < largest] or [i for i in range(1, amount) if counts[i] < limit]
        whole, left = sum([weights[i] for i in free]), spare
        for i in free:
            addition = min(limit - counts[i], max(1, left * weights[i] // whole), spare)
            counts[i] = counts[i] + addition
            spare = spare - addition
    return np.array(counts)


def gaussian(rng, shape, width, bound, cuts=(), dtype=jnp.bfloat16):
    loudness = shard_levels(rng, shape, cuts, -0.22, 0.18) if cuts else 1.0
    entries = jax.random.normal(rng, shape, jnp.float32) * width * loudness
    return jnp.minimum(jnp.maximum(entries, -bound), bound).astype(dtype)


def setup_inputs(seed: int = 0) -> dict:
    splits = jax.random.split(jax.random.key(seed), 11)
    state = gaussian(splits[0], (2, KF, LEV, NX, NY), 1.0, 6.0, ((0, 2), (3, 8), (4, 2)), jnp.float32)
    diffusion = jnp.clip(jnp.exp(math.log(0.15) - 1.609438 * jax.random.uniform(splits[1], (2, NX, NY), jnp.float32) ** shard_levels(splits[1], (2, NX, NY), ((0, 2), (1, 8), (2, 2)), -0.2, 0.2)), 0.03, 0.15)
    vertical = jnp.clip(jnp.exp(math.log(0.1) - 2.3025851 * jax.random.uniform(splits[2], (2, LEV), jnp.float32) ** shard_levels(splits[2], (2, LEV), ((0, 2),), -0.2, 0.2)), 0.01, 0.1)
    coupling = jnp.clip(jnp.exp(math.log(0.2) - 2.3025851 * jax.random.uniform(splits[3], (2, NX, NY), jnp.float32) ** shard_levels(splits[3], (2, NX, NY), ((0, 2), (1, 8), (2, 2)), -0.2, 0.2)), 0.02, 0.2)
    land_sea = set_ends((jax.random.randint(splits[4], (2, NX, NY), 0, 10) < 7).astype(jnp.int32), jax.random.fold_in(splits[4], 1), 0, 1)
    route_tile_keys = jax.random.split(jax.random.fold_in(splits[5], 1), 2 * NT * P_SIZE // P_SIZE)
    route_tile_turns = jax.random.permutation(jax.random.fold_in(splits[5], 3), 2 * NT * P_SIZE // P_SIZE)
    route_tile = jax.vmap(lambda own, number: deal_out(jax.random.fold_in(splits[5], 2), own, number, P_SIZE, NT, 1, SLOTS, 2))(route_tile_keys, route_tile_turns).reshape((2, NT, P_SIZE, 1))
    route_src = set_ends(jax.random.randint(splits[6], (2, NT, P_SIZE), 0, NB), jax.random.fold_in(splits[6], 1), 0, NB - 1).astype(jnp.int32)
    route_dst = set_ends(jax.random.randint(splits[7], (2, NT, P_SIZE), 0, NB), jax.random.fold_in(splits[7], 1), 0, NB - 1).astype(jnp.int32)
    pair_cols = set_ends(jax.random.randint(splits[8], (2, NT, P_SIZE), 64, 129), jax.random.fold_in(splits[8], 1), 64, 128).astype(jnp.int32)
    intersection = jnp.clip(0.03125 * jax.random.uniform(splits[9], (2, NT, P_SIZE, BLK, BLK), jnp.float32) ** shard_levels(splits[9], (2, NT, P_SIZE, BLK, BLK), ((0, 2), (1, 16)), -0.2, 0.2), 0.0, 0.03125).astype(jnp.bfloat16)
    return dict(state=state, diffusion=diffusion, vertical=vertical, coupling=coupling, land_sea=land_sea, route_tile=route_tile, route_src=route_src, route_dst=route_dst, pair_cols=pair_cols, intersection=intersection)


def advance(padded, diff_num, mix_num, couple_num, gate, target):
    center = padded[:, :, 1:-1, 1:-1]
    lap_h = padded[:, :, 2:, 1:-1] + padded[:, :, :-2, 1:-1] + padded[:, :, 1:-1, 2:] + padded[:, :, 1:-1, :-2] - 4.0 * center
    column = jnp.concatenate([center[:, :1], center, center[:, -1:]], axis=1)
    lap_v = column[:, 2:] - 2.0 * center + column[:, :-2]
    tend = diff_num[None, None] * lap_h + mix_num[None, :, None, None] * lap_v
    force = couple_num[None] * (target - center[:, 0])
    tend = jnp.concatenate([tend[:, :1] + force[:, None], tend[:, 1:]], axis=1)
    return center + gate[None, None] * tend


def to_tiles(field):
    return field.reshape(KF, N_GX, CX, N_GY, CY).transpose(1, 3, 0, 2, 4).reshape(NT, KF, NB, BLK)


def from_tiles(tiled):
    return tiled.reshape(N_GX, N_GY, KF, CX, CY).transpose(2, 0, 3, 1, 4).reshape(KF, NX, NY)


def remap_one(fields_s, tile_s, src_s, dst_s, cols_s, weights_s):
    surface = fields_s[:, 0].astype(jnp.bfloat16)
    tiled = to_tiles(surface)
    lanes = jnp.arange(BLK)

    def per_tile(packed):
        blocks, sources, weights, cols = packed
        picked = blocks[:, sources].astype(jnp.float32)
        contrib = jnp.einsum('pij,kpj->pki', weights.astype(jnp.float32), picked, precision=lax.Precision.HIGHEST)
        rowmask = (lanes[None, :] < cols[:, None]).astype(jnp.float32)
        return contrib * rowmask[:, None, :]

    contrib = lax.map(per_tile, (tiled, src_s, weights_s, cols_s))
    segment = (tile_s[:, :, 0] * NB + dst_s).reshape(-1)
    summed = jax.ops.segment_sum(contrib.reshape(NT * P_SIZE, KF, BLK), segment, num_segments=NT * NB)
    summed = summed.reshape(NT, NB, KF, BLK).transpose(0, 2, 1, 3)
    return from_tiles(summed)


def reference(state, diffusion, vertical, coupling, land_sea, route_tile, route_src, route_dst, pair_cols, intersection):
    fields = [state[0], state[1]]
    sea = land_sea.astype(jnp.float32)
    gates = [jnp.ones_like(sea[0]), sea[1]]
    for interval in range(INTERVALS):
        sent = [remap_one(fields[s], route_tile[s], route_src[s], route_dst[s], pair_cols[s], intersection[s]) for s in range(2)]
        arrived = [sent[1], sent[0]]
        for s in range(2):
            target = sea[s][None] * arrived[s]
            current = fields[s]
            for sub in range(SUBSTEPS):
                padded = jnp.pad(current, ((0, 0), (0, 0), (1, 1), (1, 1)), mode='wrap')
                current = advance(padded, diffusion[s], vertical[s], coupling[s], gates[s], target)
            fields[s] = current
    return jnp.stack(fields)
```

```python
import functools

import jax
import jax.numpy as jnp
from jax import lax
from jax.experimental import pallas as pl
from jax.experimental.pallas import tpu as pltpu
from jax.sharding import PartitionSpec as P

SUBSTEPS = 3
INTERVALS = 2
MESH = pl.DeviceIdType.MESH
HIGHEST = lax.Precision.HIGHEST
TOP = 8
SLAB = 8
LANES = 128
CHUNK = 4


def split_rows(value):
    first = value.astype(jnp.bfloat16)
    rest = value - first.astype(jnp.float32)
    second = rest.astype(jnp.bfloat16)
    third = (rest - second.astype(jnp.float32)).astype(jnp.bfloat16)
    return first, second, third


def pick(onehot, value):
    total = None
    for part in split_rows(value):
        term = jnp.dot(onehot, part, preferred_element_type=jnp.float32)
        total = term if total is None else total + term
    return total


def kernel(
    dims,
    state_ref,
    diff_ref,
    mix_ref,
    couple_ref,
    sea_ref,
    tile_ref,
    src_ref,
    dst_ref,
    cols_ref,
    weight_ref,
    out_ref,
    state_v,
    weight_v,
    *rest,
):
    n_gx, n_gy, tiles, rows, pairs, tracers, levels, width = dims
    count = INTERVALS * SUBSTEPS
    fields = rest[:count]
    rest = rest[count:]
    slabs = rest[: INTERVALS * (SUBSTEPS - 1)]
    rest = rest[INTERVALS * (SUBSTEPS - 1) :]
    pack_out = rest[:count]
    pack_in = rest[count : 2 * count]
    rest = rest[2 * count :]
    slab_count = INTERVALS * (SUBSTEPS - 1) + 1
    slab_out = rest[:slab_count]
    slab_in = rest[slab_count : 2 * slab_count]
    rest = rest[2 * slab_count :]
    sends = rest[:INTERVALS]
    recvs = rest[INTERVALS : 2 * INTERVALS]
    rest = rest[2 * INTERVALS :]
    (
        label_out,
        label_in,
        surf,
        contrib,
        gate_diff,
        gate_couple,
        gate_ref,
        mix_v,
        goal,
        onehot_v,
        dense_v,
        load_sem,
        halo_send,
        halo_recv,
        route_send,
        route_recv,
    ) = rest

    comp = lax.axis_index("comp")
    gx = lax.axis_index("gx")
    gy = lax.axis_index("gy")
    other = 1 - comp
    mine = gx * n_gy + gy
    right = (comp, lax.rem(gx + 1, n_gx), gy)
    left = (comp, lax.rem(gx + n_gx - 1, n_gx), gy)
    across = (comp, gx, lax.rem(gy + 1, n_gy))

    state_copy = pltpu.make_async_copy(state_ref, state_v, load_sem.at[0])
    state_copy.start()
    weight_copy = pltpu.make_async_copy(weight_ref, weight_v, load_sem.at[1])
    weight_copy.start()

    def peer(step):
        tile = lax.rem(mine + step, tiles)
        return tile, (other, tile // n_gy, lax.rem(tile, n_gy))

    barrier = pltpu.get_barrier_semaphore()
    for device in (right, left, across):
        pl.semaphore_signal(barrier, inc=1, device_id=device, device_id_type=MESH)

    def greet(step, carry):
        pl.semaphore_signal(barrier, inc=1, device_id=peer(step)[1], device_id_type=MESH)
        return carry

    lax.fori_loop(0, tiles, greet, 0)

    dest_col = jnp.broadcast_to(tile_ref[0, 0], (pairs, pairs))
    sub_ids = lax.broadcasted_iota(jnp.int32, (pairs, pairs), 0)
    lane_ids = lax.broadcasted_iota(jnp.int32, (pairs, pairs), 1)
    dest_row = jnp.sum(
        jnp.where(sub_ids == lane_ids, dest_col, 0).astype(jnp.float32), axis=0, keepdims=True
    )
    earlier = (dest_col.astype(jnp.float32) == dest_row) & (sub_ids < lane_ids)
    rank = jnp.sum(jnp.where(earlier, 1.0, 0.0), axis=0, keepdims=True)
    place = (dest_row * rows + rank).astype(jnp.int32)
    slot_ids = lax.broadcasted_iota(jnp.int32, (tiles * rows, pairs), 0)
    taken = slot_ids == place
    onehot_v[...] = jnp.where(taken, 1.0, 0.0).astype(jnp.bfloat16)
    labels = jnp.sum(
        jnp.where(taken, (dst_ref[0] + 1).astype(jnp.float32), 0.0), axis=1, keepdims=True
    )
    label_out[...] = jnp.broadcast_to(labels, (tiles * rows, LANES)).reshape(tiles, rows, LANES)

    sea = sea_ref[0].astype(jnp.float32)
    gate = jnp.where(comp == 1, sea, jnp.ones_like(sea))
    gate_ref[...] = gate
    gate_diff[...] = gate * diff_ref[0]
    gate_couple[...] = gate * couple_ref[0]
    level_a = lax.broadcasted_iota(jnp.int32, (levels, levels), 0)
    level_b = lax.broadcasted_iota(jnp.int32, (levels, levels), 1)
    mix_col = jnp.sum(
        jnp.where(level_a == level_b, jnp.broadcast_to(mix_ref[...], (levels, levels)), 0.0),
        axis=1,
        keepdims=True,
    )
    mix_v[...] = jnp.broadcast_to(mix_col, (levels, LANES))
    surf[...] = jnp.zeros(surf.shape, jnp.float32)

    def lane_of(height):
        return lax.broadcasted_iota(jnp.int32, (height, LANES), 1)

    def packed_lane(acc, value, place_j, height):
        turned = pltpu.roll(value, 2 * place_j + 1, 1)
        return jnp.where(lane_of(height) // 2 == place_j, turned, acc)

    def over_columns(body, acc):
        def step(chunk, acc):
            for i in range(CHUNK):
                for f in range(tracers):
                    acc = body(f, chunk * CHUNK + i, acc)
            return acc

        return lax.fori_loop(0, width // CHUNK, step, acc)

    def exchange(number, to_right, to_left, packs):
        copies = []
        for i, (src, dst, device) in enumerate(
            ((to_right[0], to_right[1], right), (to_left[0], to_left[1], left), (packs[0], packs[1], across))
        ):
            copy = pltpu.make_async_remote_copy(
                src_ref=src,
                dst_ref=dst,
                send_sem=halo_send.at[number, i],
                recv_sem=halo_recv.at[number, i],
                device_id=device,
                device_id_type=MESH,
            )
            copy.start()
            copies.append(copy)
        return copies

    def x_sides(buf, low, high):
        span = pl.ds(low, high - low)
        to_right = (buf.at[:, width, span, :], buf.at[:, 0, span, :])
        to_left = (buf.at[:, 1, span, :], buf.at[:, width + 1, span, :])
        return to_right, to_left

    started = []
    numbers = iter(range(64))

    def send_halo(buf, low, high, out, into):
        copies = exchange(next(numbers), *x_sides(buf, low, high), (out, into))
        started.extend(copies)
        return copies

    def stencil(buf, f, x, low, height, halo):
        center = buf[f, x + 1, low : low + height]
        after = buf[f, x + 2, low : low + height]
        before = buf[f, x, low : low + height]
        above = buf[f, x + 1, low - 1 : low - 1 + height]
        below = buf[f, x + 1, low + 1 : low + 1 + height]
        j = f * width + x
        turned = pltpu.roll(halo, LANES - 1 - 2 * j, 1)
        lanes = lane_of(height)
        north = pltpu.roll(jnp.where(lanes == 0, turned, center), LANES - 1, 1)
        south = pltpu.roll(jnp.where(lanes == LANES - 1, turned, center), 1, 1)
        lap_h = (after + before) + (north + south) - 4.0 * center
        lap_v = (below + above) - 2.0 * center
        row = pl.ds(x, 1)
        gd = jnp.broadcast_to(gate_diff[row, :], (height, LANES))
        gv = jnp.broadcast_to(gate_ref[row, :], (height, LANES)) * mix_v[low - TOP : low - TOP + height]
        return center, center + (gd * lap_h + gv * lap_v)

    def with_ends(buf, f, x, value, height):
        buf[f, x + 1, TOP - 1 : TOP] = value[0:1]
        buf[f, x + 1, TOP + height : TOP + height + 1] = value[height - 1 : height]

    pl.semaphore_wait(barrier, tiles + 3)

    def send_labels(step, carry):
        tile, device = peer(step)
        pltpu.make_async_remote_copy(
            src_ref=label_out.at[tile],
            dst_ref=label_in.at[mine],
            send_sem=route_send.at[INTERVALS],
            recv_sem=route_recv.at[INTERVALS],
            device_id=device,
            device_id_type=MESH,
        ).start()
        return carry

    lax.fori_loop(0, tiles, send_labels, 0)

    state_copy.wait()

    def load(f, x, acc):
        value = state_v[pl.ds(f * levels * width + x, levels, stride=width), :]
        fields[0][f, x + 1, TOP : TOP + levels] = value
        with_ends(fields[0], f, x, value, levels)
        surf[x, f : f + 1] = value[0:1]
        return packed_lane(acc, value, f * width + x, levels)

    pack_out[0][...] = over_columns(load, jnp.zeros((levels, LANES), jnp.float32))
    whole = (TOP, TOP + levels)
    pending = send_halo(fields[0], *whole, pack_out[0], pack_in[0])
    weight_copy.wait()

    def remap(interval):
        lanes = lane_of(SLAB)

        def one(group, carry):
            for i in range(8):
                p = group * 8 + i
                left_side = surf[src_ref[0, 0, p]].astype(jnp.bfloat16)
                got = lax.dot_general(
                    left_side,
                    weight_v[p],
                    (((1,), (1,)), ((), ())),
                    preferred_element_type=jnp.float32,
                )
                got = jnp.where(lanes < cols_ref[0, 0, p], got, 0.0)
                contrib[pl.ds(pl.multiple_of(p * 8, 8), 8), :] = got
            return carry

        lax.fori_loop(0, pairs // 8, one, 0)
        onehot = onehot_v[...]
        for f in range(tracers):
            value = contrib[pl.ds(f, pairs, stride=8), :]
            sends[interval][:, :, f * LANES : (f + 1) * LANES] = pick(onehot, value).reshape(
                tiles, rows, LANES
            )

        def post(step, carry):
            tile, device = peer(step)
            pltpu.make_async_remote_copy(
                src_ref=sends[interval].at[tile],
                dst_ref=recvs[interval].at[mine],
                send_sem=route_send.at[interval],
                recv_sem=route_recv.at[interval],
                device_id=device,
                device_id_type=MESH,
            ).start()
            return carry

        lax.fori_loop(0, tiles, post, 0)

    def wait_whole(ref, sem):
        pltpu.make_async_copy(ref, ref, sem).wait()

    zeros = jnp.zeros((levels, LANES), jnp.float32)
    slab_zeros = jnp.zeros((SLAB, LANES), jnp.float32)
    slab_number = 0
    slab_pending = []
    for interval in range(INTERVALS):
        final = interval == INTERVALS - 1
        remap(interval)
        first = interval * SUBSTEPS
        for sub in range(SUBSTEPS):
            for copy in pending:
                copy.wait_recv()
            pending = []
            if sub == 0:
                for copy in slab_pending:
                    copy.wait_recv()
                entry_slab = slab_in[slab_number - 1] if interval > 0 else None
                slab_pending = []
            buf = fields[first + sub]
            pack = pack_in[first + sub]
            if sub == 0 and interval > 0:
                pack[0:SLAB, :] = entry_slab[...]
            last = sub == SUBSTEPS - 1
            low = TOP + (SLAB if last else 0)
            height = levels - (SLAB if last else 0)
            halo_low = low - TOP

            def bulk(f, x, acc):
                _, value = stencil(buf, f, x, low, height, pack[halo_low:levels, :])
                if last and final:
                    start = f * levels * width + SLAB * width + x
                    out_ref[pl.ds(start, height, stride=width), :] = value
                    return acc
                after = fields[first + sub + 1]
                after[f, x + 1, low : low + height] = value
                if last:
                    after[f, x + 1, TOP + levels : TOP + levels + 1] = value[height - 1 : height]
                else:
                    with_ends(after, f, x, value, height)
                return packed_lane(acc, value, f * width + x, height)

            if last and final:
                over_columns(bulk, 0)
            else:
                packed = over_columns(bulk, zeros[0:height])
                pack_out[first + sub + 1][halo_low:levels, :] = packed
                part = (pack_out[first + sub + 1], pack_in[first + sub + 1])
                if last:
                    part = [ref.at[pl.ds(SLAB, height), :] for ref in part]
                pending = send_halo(fields[first + sub + 1], low, low + height, *part)

        if interval == 0:
            wait_whole(label_in, route_recv.at[INTERVALS])
            got_labels = label_in[...].reshape(tiles * rows, LANES)
            block_ids = lax.broadcasted_iota(jnp.int32, (tiles * rows, LANES), 1) + 1
            named = jnp.where(got_labels == block_ids.astype(jnp.float32), 1.0, 0.0)
            dense_v[...] = jnp.transpose(named)[0:width, :].astype(jnp.bfloat16)
        wait_whole(recvs[interval], route_recv.at[interval])
        dense = dense_v[...]
        for f in range(tracers):
            value = recvs[interval][:, :, f * LANES : (f + 1) * LANES].reshape(tiles * rows, LANES)
            goal[f] = sea * pick(dense, value)

        for sub in range(SUBSTEPS):
            for copy in slab_pending:
                copy.wait_recv()
            slab_pending = []
            index = interval * (SUBSTEPS - 1) + sub - 1
            if sub == 0:
                buf = fields[first]
                halo_ref = pack_in[first]
            else:
                buf = slabs[index]
                halo_ref = slab_in[slab_number - 1]
            last = sub == SUBSTEPS - 1

            def near(f, x, acc):
                center, value = stencil(buf, f, x, TOP, SLAB, halo_ref[0:SLAB, :])
                row = pl.ds(x, 1)
                force = jnp.broadcast_to(gate_couple[row, :], (SLAB, LANES)) * (
                    jnp.broadcast_to(goal[f, row, :], (SLAB, LANES)) - center
                )
                sub_row = lax.broadcasted_iota(jnp.int32, (SLAB, LANES), 0)
                value = value + jnp.where(sub_row == 0, force, 0.0)
                if last and final:
                    out_ref[pl.ds(f * levels * width + x, SLAB, stride=width), :] = value
                    return acc
                if last:
                    after = fields[first + SUBSTEPS]
                    surf[x, f : f + 1] = value[0:1]
                else:
                    after = slabs[index + 1]
                    after[f, x + 1, TOP + SLAB : TOP + SLAB + 1] = fields[first + sub + 1][
                        f, x + 1, TOP + SLAB : TOP + SLAB + 1
                    ]
                after[f, x + 1, TOP : TOP + SLAB] = value
                after[f, x + 1, TOP - 1 : TOP] = value[0:1]
                return packed_lane(acc, value, f * width + x, SLAB)

            if last and final:
                over_columns(near, 0)
            else:
                slab_out[slab_number][...] = over_columns(near, slab_zeros)
                after = fields[first + SUBSTEPS] if last else slabs[index + 1]
                slab_pending = send_halo(
                    after, TOP, TOP + SLAB, slab_out[slab_number], slab_in[slab_number]
                )
                slab_number += 1

    for copy in started:
        copy.wait_send()
    for interval in range(INTERVALS):
        wait_whole(sends[interval], route_send.at[interval])
    wait_whole(label_out, route_send.at[INTERVALS])


def body(
    n_gx,
    n_gy,
    state,
    diffusion,
    vertical,
    coupling,
    land_sea,
    route_tile,
    route_src,
    route_dst,
    pair_cols,
    intersection,
):
    _, tracers, levels, width, lanes = state.shape
    assert lanes == LANES and n_gy == 2 and 2 * tracers * width <= LANES
    tiles = n_gx * n_gy
    pairs = route_src.shape[2]
    slots = max(2, 2 * pairs // tiles)
    rows = -(-slots // 8) * 8
    dims = (n_gx, n_gy, tiles, rows, pairs, tracers, levels, width)
    count = INTERVALS * SUBSTEPS
    slab_count = INTERVALS * (SUBSTEPS - 1) + 1
    f32 = jnp.float32
    scratch = [
        pltpu.VMEM((tracers * levels * width, LANES), f32),
        pltpu.VMEM(intersection.shape[2:], jnp.bfloat16),
    ]
    scratch += [pltpu.VMEM((tracers, width + 2, TOP + levels + 8, LANES), f32)] * count
    scratch += [pltpu.VMEM((tracers, width + 2, TOP + SLAB + 8, LANES), f32)] * (
        INTERVALS * (SUBSTEPS - 1)
    )
    scratch += [pltpu.VMEM((levels, LANES), f32)] * (2 * count)
    scratch += [pltpu.VMEM((SLAB, LANES), f32)] * (2 * slab_count)
    scratch += [pltpu.VMEM((tiles, rows, tracers * LANES), f32)] * (2 * INTERVALS)
    scratch += [
        pltpu.VMEM((tiles, rows, LANES), f32),
        pltpu.VMEM((tiles, rows, LANES), f32),
        pltpu.VMEM((width, 8, LANES), f32),
        pltpu.VMEM((pairs * 8, LANES), f32),
        pltpu.VMEM((width, LANES), f32),
        pltpu.VMEM((width, LANES), f32),
        pltpu.VMEM((width, LANES), f32),
        pltpu.VMEM((levels, LANES), f32),
        pltpu.VMEM((tracers, width, LANES), f32),
        pltpu.VMEM((tiles * rows, pairs), jnp.bfloat16),
        pltpu.VMEM((width, tiles * rows), jnp.bfloat16),
        pltpu.SemaphoreType.DMA((2,)),
        pltpu.SemaphoreType.DMA((count + slab_count, 3)),
        pltpu.SemaphoreType.DMA((count + slab_count, 3)),
        pltpu.SemaphoreType.DMA((INTERVALS + 1,)),
        pltpu.SemaphoreType.DMA((INTERVALS + 1,)),
    ]
    vmem = pl.BlockSpec(memory_space=pltpu.VMEM)
    smem = pl.BlockSpec(memory_space=pltpu.SMEM)
    hbm = pl.BlockSpec(memory_space=pl.ANY)
    out = pl.pallas_call(
        functools.partial(kernel, dims),
        out_shape=jax.ShapeDtypeStruct((tracers * levels * width, LANES), f32),
        in_specs=[hbm, vmem, vmem, vmem, vmem, vmem, smem, vmem, smem, hbm],
        out_specs=vmem,
        scratch_shapes=scratch,
        compiler_params=pltpu.CompilerParams(
            collective_id=0, has_side_effects=True, vmem_limit_bytes=48 * 2**20
        ),
        cost_estimate=pl.CostEstimate(flops=60_000_000, bytes_accessed=5_000_000, transcendentals=0),
        name="coupled_columns",
    )(
        state.reshape(tracers * levels * width, LANES),
        diffusion,
        vertical,
        coupling,
        land_sea,
        route_tile,
        route_src,
        route_dst,
        pair_cols,
        intersection.reshape(intersection.shape[2:]),
    )
    return out.reshape(state.shape)


def solution(mesh):
    in_specs = (
        P("comp", None, None, "gx", "gy"),
        P("comp", "gx", "gy"),
        P("comp", None),
        P("comp", "gx", "gy"),
        P("comp", "gx", "gy"),
        P("comp", ("gx", "gy"), None, None),
        P("comp", ("gx", "gy"), None),
        P("comp", ("gx", "gy"), None),
        P("comp", ("gx", "gy"), None),
        P("comp", ("gx", "gy"), None, None, None),
    )
    out_specs = P("comp", None, None, "gx", "gy")
    run = functools.partial(body, mesh.shape["gx"], mesh.shape["gy"])
    return jax.shard_map(run, mesh=mesh, in_specs=in_specs, out_specs=out_specs, check_vma=False)
```

```python
import functools

import jax
import jax.numpy as jnp
from jax import lax
from jax.experimental import pallas as pl
from jax.experimental.pallas import tpu as pltpu
from jax.sharding import PartitionSpec as P

SUBSTEPS = 3
INTERVALS = 2
MESH = pl.DeviceIdType.MESH
HIGHEST = lax.Precision.HIGHEST
TOP = 8
SLAB = 8
LANES = 128
CHUNK = 4


def split_rows(value):
    first = value.astype(jnp.bfloat16)
    rest = value - first.astype(jnp.float32)
    second = rest.astype(jnp.bfloat16)
    third = (rest - second.astype(jnp.float32)).astype(jnp.bfloat16)
    return first, second, third


def pick(onehot, value):
    total = None
    for part in split_rows(value):
        term = jnp.dot(onehot, part, preferred_element_type=jnp.float32)
        total = term if total is None else total + term
    return total


def kernel(
    dims,
    state_ref,
    diff_hbm,
    mix_hbm,
    couple_hbm,
    sea_hbm,
    tile_hbm,
    src_hbm,
    dst_hbm,
    cols_hbm,
    weight_ref,
    out_hbm,
    state_v,
    weight_v,
    out_ref,
    diff_ref,
    mix_ref,
    couple_ref,
    sea_ref,
    tile_ref,
    src_ref,
    dst_ref,
    cols_ref,
    *rest,
):
    n_gx, n_gy, tiles, rows, pairs, tracers, levels, width = dims
    count = INTERVALS * SUBSTEPS
    groups = levels // SLAB
    per_row = LANES // (2 * width)
    pack_rows = -(-groups // per_row) * SLAB
    fields = rest[:count]
    rest = rest[count:]
    slabs = rest[: INTERVALS * (SUBSTEPS - 1)]
    rest = rest[INTERVALS * (SUBSTEPS - 1) :]
    pack_out = rest[: count * tracers]
    pack_in = rest[count * tracers : 2 * count * tracers]
    rest = rest[2 * count * tracers :]
    slab_count = INTERVALS * (SUBSTEPS - 1) + 1
    slab_out = rest[:slab_count]
    slab_in = rest[slab_count : 2 * slab_count]
    rest = rest[2 * slab_count :]
    sends = rest[:INTERVALS]
    recvs = rest[INTERVALS : 2 * INTERVALS]
    rest = rest[2 * INTERVALS :]
    (
        label_out,
        label_in,
        surf,
        contrib,
        gate_diff,
        gate_couple,
        gate_ref,
        mix_v,
        goal,
        onehot_v,
        dense_v,
        load_sem,
        halo_send,
        halo_recv,
        route_send,
        route_recv,
        out_sem,
    ) = rest

    comp = lax.axis_index("comp")
    gx = lax.axis_index("gx")
    gy = lax.axis_index("gy")
    other = 1 - comp
    mine = gx * n_gy + gy
    right = (comp, lax.rem(gx + 1, n_gx), gy)
    left = (comp, lax.rem(gx + n_gx - 1, n_gx), gy)
    across = (comp, gx, lax.rem(gy + 1, n_gy))

    loads = []
    for src, dst in (
        (tile_hbm, tile_ref),
        (dst_hbm, dst_ref),
        (state_ref, state_v),
        (sea_hbm, sea_ref),
        (diff_hbm, diff_ref),
        (couple_hbm, couple_ref),
        (mix_hbm, mix_ref),
        (src_hbm, src_ref),
        (cols_hbm, cols_ref),
        (weight_ref, weight_v),
    ):
        copy = pltpu.make_async_copy(src, dst, load_sem.at[len(loads)])
        copy.start()
        loads.append(copy)

    def peer(step):
        tile = lax.rem(mine + step, tiles)
        return tile, (other, tile // n_gy, lax.rem(tile, n_gy))

    barrier = pltpu.get_barrier_semaphore()
    for device in (right, left, across):
        pl.semaphore_signal(barrier, inc=1, device_id=device, device_id_type=MESH)

    def greet(step, carry):
        pl.semaphore_signal(barrier, inc=1, device_id=peer(step)[1], device_id_type=MESH)
        return carry

    lax.fori_loop(0, tiles, greet, 0)

    loads[0].wait()
    loads[1].wait()
    sub_ids = lax.broadcasted_iota(jnp.int32, (pairs, pairs), 0)
    lane_ids = lax.broadcasted_iota(jnp.int32, (pairs, pairs), 1)
    dest_row = tile_ref[0].astype(jnp.float32)
    dest_wide = jnp.broadcast_to(dest_row, (pairs, pairs))
    dest_col = jnp.sum(jnp.where(sub_ids == lane_ids, dest_wide, 0.0), axis=1, keepdims=True)
    same = dest_col == dest_wide
    rank_row = jnp.sum(jnp.where(same & (sub_ids < lane_ids), 1.0, 0.0), axis=0, keepdims=True)
    rank_col = jnp.sum(jnp.where(same & (lane_ids < sub_ids), 1.0, 0.0), axis=1, keepdims=True)
    place = (dest_row * rows + rank_row).astype(jnp.int32)
    slot_ids = lax.broadcasted_iota(jnp.int32, (tiles * rows, pairs), 0)
    onehot_v[...] = jnp.where(slot_ids == place, 1.0, 0.0).astype(jnp.bfloat16)
    tile_ids = lax.broadcasted_iota(jnp.int32, (tiles, pairs), 0).astype(jnp.float32)
    named = jnp.where(tile_ids == dest_row, (dst_ref[0] + 1).astype(jnp.float32), 0.0)
    slot_lane = lax.broadcasted_iota(jnp.int32, (pairs, LANES), 1).astype(jnp.float32)
    ranked = jnp.where(slot_lane == rank_col, 1.0, 0.0)
    label_out[...] = jnp.dot(
        named.astype(jnp.bfloat16), ranked.astype(jnp.bfloat16), preferred_element_type=jnp.float32
    ).reshape(tiles, 1, LANES)

    surf[...] = jnp.zeros(surf.shape, jnp.float32)

    def lane_of(height):
        return lax.broadcasted_iota(jnp.int32, (height, LANES), 1)

    pairs_lane = lane_of(SLAB) // 2

    def pack_tile(acc, value, j):
        return jnp.where(pairs_lane == j, pltpu.roll(value, 2 * j + 1, 1), acc)

    def unpack_tile(value, j):
        return pltpu.roll(value, LANES - 1 - 2 * j, 1)

    def pack_column(acc, value, x, skip):
        acc = list(acc)
        for g in range(skip, groups):
            part = value[(g - skip) * SLAB : (g - skip + 1) * SLAB]
            acc[g // per_row] = pack_tile(acc[g // per_row], part, (g % per_row) * width + x)
        return tuple(acc)

    def unpack_column(ref, x, skip):
        parts = []
        for g in range(skip, groups):
            low = (g // per_row) * SLAB
            parts.append(unpack_tile(ref[low : low + SLAB, :], (g % per_row) * width + x))
        return parts

    def exchange(number, to_right, to_left, packs):
        copies = []
        for i, (src, dst, device) in enumerate(
            ((packs[0], packs[1], across), (to_right[0], to_right[1], right), (to_left[0], to_left[1], left))
        ):
            copy = pltpu.make_async_remote_copy(
                src_ref=src,
                dst_ref=dst,
                send_sem=halo_send.at[number, i],
                recv_sem=halo_recv.at[number, i],
                device_id=device,
                device_id_type=MESH,
            )
            copy.start()
            copies.append(copy)
        return copies

    def x_sides(buf, f, low, high):
        span = pl.ds(low, high - low)
        to_right = (buf.at[f, width, span, :], buf.at[f, 0, span, :])
        to_left = (buf.at[f, 1, span, :], buf.at[f, width + 1, span, :])
        return to_right, to_left

    started = []
    numbers = iter(range(64))

    def send_halo(buf, f, low, high, out, into):
        copies = exchange(next(numbers), *x_sides(buf, f, low, high), (out, into))
        started.extend(copies)
        return copies

    def stencil(buf, f, x, low, height, turned):
        center = buf[f, x + 1, low : low + height]
        after = buf[f, x + 2, low : low + height]
        before = buf[f, x, low : low + height]
        above = buf[f, x + 1, low - 1 : low - 1 + height]
        below = buf[f, x + 1, low + 1 : low + 1 + height]
        lanes = lane_of(height)
        north = pltpu.roll(jnp.where(lanes == 0, turned, center), LANES - 1, 1)
        south = pltpu.roll(jnp.where(lanes == LANES - 1, turned, center), 1, 1)
        lap_h = (after + before) + (north + south) - 4.0 * center
        lap_v = (below + above) - 2.0 * center
        row = pl.ds(x, 1)
        gd = jnp.broadcast_to(gate_diff[row, :], (height, LANES))
        gv = jnp.broadcast_to(gate_ref[row, :], (height, LANES)) * mix_v[low - TOP : low - TOP + height]
        return center, center + (gd * lap_h + gv * lap_v)

    def with_ends(buf, f, x, value, height):
        buf[f, x + 1, TOP - 1 : TOP] = value[0:1]
        buf[f, x + 1, TOP + height : TOP + height + 1] = value[height - 1 : height]

    pl.semaphore_wait(barrier, tiles + 3)

    def post_all(source, target, number):
        def post(step, carry):
            tile, device = peer(step)
            pltpu.make_async_remote_copy(
                src_ref=source.at[tile],
                dst_ref=target.at[mine],
                send_sem=route_send.at[number],
                recv_sem=route_recv.at[number],
                device_id=device,
                device_id_type=MESH,
            ).start()
            return carry

        lax.fori_loop(0, tiles, post, 0)

    zero = jnp.zeros((SLAB, LANES), jnp.float32)
    empty = (zero,) * (pack_rows // SLAB)

    def store_pack(ref, acc):
        for i, part in enumerate(acc):
            ref[i * SLAB : (i + 1) * SLAB, :] = part

    loads[2].wait()
    pending = []
    for f in range(tracers):

        def load(chunk, acc):
            for i in range(CHUNK):
                x = chunk * CHUNK + i
                value = state_v[pl.ds(f * levels * width + x, levels, stride=width), :]
                fields[0][f, x + 1, TOP : TOP + levels] = value
                with_ends(fields[0], f, x, value, levels)
                surf[x, f : f + 1] = value[0:1]
                acc = pack_column(acc, value, x, 0)
            return acc

        store_pack(pack_out[f], lax.fori_loop(0, width // CHUNK, load, empty))
        pending.append(send_halo(fields[0], f, TOP, TOP + levels, pack_out[f], pack_in[f]))
    post_all(label_out, label_in, INTERVALS)

    for copy in loads[3:]:
        copy.wait()
    sea = sea_ref[0].astype(jnp.float32)
    gate = jnp.where(comp == 1, sea, jnp.ones_like(sea))
    gate_ref[...] = gate
    gate_diff[...] = gate * diff_ref[0]
    gate_couple[...] = gate * couple_ref[0]
    level_a = lax.broadcasted_iota(jnp.int32, (levels, levels), 0)
    level_b = lax.broadcasted_iota(jnp.int32, (levels, levels), 1)
    mix_col = jnp.sum(
        jnp.where(level_a == level_b, jnp.broadcast_to(mix_ref[...], (levels, levels)), 0.0),
        axis=1,
        keepdims=True,
    )
    mix_v[...] = jnp.broadcast_to(mix_col, (levels, LANES))

    def remap(interval):
        lanes = lane_of(SLAB)

        def one(group, carry):
            for i in range(16):
                p = group * 16 + i
                left_side = surf[src_ref[0, 0, p]].astype(jnp.bfloat16)
                got = lax.dot_general(
                    left_side,
                    weight_v[p],
                    (((1,), (1,)), ((), ())),
                    preferred_element_type=jnp.float32,
                )
                got = jnp.where(lanes < cols_ref[0, 0, p], got, 0.0)
                contrib[pl.ds(pl.multiple_of(p * 8, 8), 8), :] = got
            return carry

        lax.fori_loop(0, pairs // 16, one, 0)
        onehot = onehot_v[...]
        for f in range(tracers):
            value = contrib[pl.ds(f, pairs, stride=8), :]
            sends[interval][:, :, f * LANES : (f + 1) * LANES] = pick(onehot, value).reshape(
                tiles, rows, LANES
            )
        post_all(sends[interval], recvs[interval], interval)

    def wait_whole(ref, sem):
        pltpu.make_async_copy(ref, ref, sem).wait()

    out_copies = []

    def write_out(f, low, high):
        span = pl.ds(f * levels * width + low * width, (high - low) * width)
        copy = pltpu.make_async_copy(
            out_ref.at[span, :], out_hbm.at[span, :], out_sem.at[len(out_copies)]
        )
        copy.start()
        out_copies.append(copy)

    inner = max(c for c in range(1, 9) if (width - 2) % c == 0)
    slab_number = 0
    slab_pending = []
    for interval in range(INTERVALS):
        final = interval == INTERVALS - 1
        first = interval * SUBSTEPS
        remap(interval)

        def bulk_step(sub, f):
            buf = fields[first + sub]
            after = None if final and sub == SUBSTEPS - 1 else fields[first + sub + 1]
            pack = pack_in[(first + sub) * tracers + f]
            fresh = sub == 0 and interval > 0
            last = sub == SUBSTEPS - 1
            skip = 1 if last else 0
            low = TOP + skip * SLAB
            height = levels - skip * SLAB
            entry = slab_in[slab_number - 1] if fresh else None

            def column(x, acc):
                parts = unpack_column(pack, x, skip)
                if fresh:
                    parts[0] = unpack_tile(entry[...], f * width + x)
                turned = jnp.concatenate(parts, axis=0)
                _, value = stencil(buf, f, x, low, height, turned)
                if after is None:
                    start = f * levels * width + SLAB * width + x
                    out_ref[pl.ds(start, height, stride=width), :] = value
                    return acc
                after[f, x + 1, low : low + height] = value
                if last:
                    after[f, x + 1, TOP + levels : TOP + levels + 1] = value[height - 1 : height]
                else:
                    with_ends(after, f, x, value, height)
                return pack_column(acc, value, x, skip)

            def chunk(step, acc):
                for i in range(inner):
                    acc = column(1 + step * inner + i, acc)
                return acc

            copies = pending[f]
            copies[0].wait_recv()
            acc = lax.fori_loop(0, (width - 2) // inner, chunk, empty)
            copies[1].wait_recv()
            copies[2].wait_recv()
            acc = column(0, acc)
            acc = column(width - 1, acc)
            if after is None:
                write_out(f, SLAB, levels)
                return
            index = (first + sub + 1) * tracers + f
            store_pack(pack_out[index], acc)
            pending[f] = send_halo(after, f, low, low + height, pack_out[index], pack_in[index])

        def near_step(sub, number, waits):
            for copy in waits:
                copy.wait_recv()
            index = interval * (SUBSTEPS - 1) + sub - 1
            buf = fields[first] if sub == 0 else slabs[index]
            last = sub == SUBSTEPS - 1
            entry = None if sub == 0 and interval == 0 else slab_in[number - 1]
            after = None
            if not last:
                after = slabs[index + 1]
            elif not final:
                after = fields[first + SUBSTEPS]
            acc = zero
            for x in range(width):
                for f in range(tracers):
                    if entry is None:
                        turned = unpack_tile(pack_in[f][0:SLAB, :], x)
                    else:
                        turned = unpack_tile(entry[...], f * width + x)
                    center, value = stencil(buf, f, x, TOP, SLAB, turned)
                    force = jnp.broadcast_to(gate_couple[x : x + 1, :], (SLAB, LANES)) * (
                        jnp.broadcast_to(goal[f, x : x + 1, :], (SLAB, LANES)) - center
                    )
                    sub_row = lax.broadcasted_iota(jnp.int32, (SLAB, LANES), 0)
                    value = value + jnp.where(sub_row == 0, force, 0.0)
                    if after is None:
                        out_ref[pl.ds(f * levels * width + x, SLAB, stride=width), :] = value
                        continue
                    if last:
                        surf[x, f : f + 1] = value[0:1]
                    else:
                        after[f, x + 1, TOP + SLAB : TOP + SLAB + 1] = fields[first + sub + 1][
                            f, x + 1, TOP + SLAB : TOP + SLAB + 1
                        ]
                    after[f, x + 1, TOP : TOP + SLAB] = value
                    after[f, x + 1, TOP - 1 : TOP] = value[0:1]
                    acc = pack_tile(acc, value, f * width + x)
            if after is None:
                return []
            slab_out[number][...] = acc
            both = slice(None)
            return send_halo(after, both, TOP, TOP + SLAB, slab_out[number], slab_in[number])

        for copy in slab_pending:
            copy.wait_recv()
        slab_pending = []
        for sub in range(SUBSTEPS - 1):
            for f in range(tracers):
                bulk_step(sub, f)

        if interval == 0:
            wait_whole(label_in, route_recv.at[INTERVALS])
            heard = label_in[...].reshape(tiles, LANES).astype(jnp.bfloat16)
            slots = tiles * rows
            spread_a = lax.broadcasted_iota(jnp.int32, (LANES, slots), 0)
            spread_b = lax.broadcasted_iota(jnp.int32, (LANES, slots), 1)
            spread = jnp.where(spread_a == spread_b % rows, 1.0, 0.0).astype(jnp.bfloat16)
            table = jnp.dot(heard, spread, preferred_element_type=jnp.float32)
            own_a = lax.broadcasted_iota(jnp.int32, (tiles, slots), 0)
            own_b = lax.broadcasted_iota(jnp.int32, (tiles, slots), 1)
            label_row = jnp.sum(jnp.where(own_a == own_b // rows, table, 0.0), axis=0, keepdims=True)
            block_ids = lax.broadcasted_iota(jnp.int32, (width, slots), 0) + 1
            dense_v[...] = jnp.where(block_ids.astype(jnp.float32) == label_row, 1.0, 0.0).astype(
                jnp.bfloat16
            )
        wait_whole(recvs[interval], route_recv.at[interval])
        dense = dense_v[...]
        for f in range(tracers):
            value = recvs[interval][:, :, f * LANES : (f + 1) * LANES].reshape(tiles * rows, LANES)
            goal[f] = sea * pick(dense, value)

        for sub in range(SUBSTEPS):
            slab_pending = near_step(sub, slab_number, slab_pending)
            if not (sub == SUBSTEPS - 1 and final):
                slab_number += 1
            if sub < tracers:
                bulk_step(SUBSTEPS - 1, sub)

    for f in range(tracers):
        write_out(f, 0, SLAB)
    for copy in started:
        copy.wait_send()
    for interval in range(INTERVALS):
        wait_whole(sends[interval], route_send.at[interval])
    wait_whole(label_out, route_send.at[INTERVALS])
    for copy in out_copies:
        copy.wait()


def body(
    n_gx,
    n_gy,
    state,
    diffusion,
    vertical,
    coupling,
    land_sea,
    route_tile,
    route_src,
    route_dst,
    pair_cols,
    intersection,
):
    _, tracers, levels, width, lanes = state.shape
    assert lanes == LANES and n_gy == 2 and 2 * tracers * width <= LANES
    tiles = n_gx * n_gy
    pairs = route_src.shape[2]
    slots = max(2, 2 * pairs // tiles)
    rows = -(-slots // 8) * 8
    dims = (n_gx, n_gy, tiles, rows, pairs, tracers, levels, width)
    count = INTERVALS * SUBSTEPS
    slab_count = INTERVALS * (SUBSTEPS - 1) + 1
    f32 = jnp.float32
    groups = levels // SLAB
    pack_rows = -(-groups // (LANES // (2 * width))) * SLAB
    halos = count * tracers + slab_count
    scratch = [
        pltpu.VMEM((tracers * levels * width, LANES), f32),
        pltpu.VMEM(intersection.shape[2:], jnp.bfloat16),
        pltpu.VMEM((tracers * levels * width, LANES), f32),
        pltpu.VMEM(diffusion.shape, f32),
        pltpu.VMEM(vertical.shape, f32),
        pltpu.VMEM(coupling.shape, f32),
        pltpu.VMEM(land_sea.shape, jnp.int32),
        pltpu.VMEM(route_src.shape, jnp.int32),
        pltpu.SMEM(route_src.shape, jnp.int32),
        pltpu.VMEM(route_dst.shape, jnp.int32),
        pltpu.SMEM(pair_cols.shape, jnp.int32),
    ]
    scratch += [pltpu.VMEM((tracers, width + 2, TOP + levels + 8, LANES), f32)] * count
    scratch += [pltpu.VMEM((tracers, width + 2, TOP + SLAB + 8, LANES), f32)] * (
        INTERVALS * (SUBSTEPS - 1)
    )
    scratch += [pltpu.VMEM((pack_rows, LANES), f32)] * (2 * count * tracers)
    scratch += [pltpu.VMEM((SLAB, LANES), f32)] * (2 * slab_count)
    scratch += [pltpu.VMEM((tiles, rows, tracers * LANES), f32)] * (2 * INTERVALS)
    scratch += [
        pltpu.VMEM((tiles, 1, LANES), f32),
        pltpu.VMEM((tiles, 1, LANES), f32),
        pltpu.VMEM((width, 8, LANES), f32),
        pltpu.VMEM((pairs * 8, LANES), f32),
        pltpu.VMEM((width, LANES), f32),
        pltpu.VMEM((width, LANES), f32),
        pltpu.VMEM((width, LANES), f32),
        pltpu.VMEM((levels, LANES), f32),
        pltpu.VMEM((tracers, width, LANES), f32),
        pltpu.VMEM((tiles * rows, pairs), jnp.bfloat16),
        pltpu.VMEM((width, tiles * rows), jnp.bfloat16),
        pltpu.SemaphoreType.DMA((10,)),
        pltpu.SemaphoreType.DMA((halos, 3)),
        pltpu.SemaphoreType.DMA((halos, 3)),
        pltpu.SemaphoreType.DMA((INTERVALS + 1,)),
        pltpu.SemaphoreType.DMA((INTERVALS + 1,)),
        pltpu.SemaphoreType.DMA((2 * tracers,)),
    ]
    hbm = pl.BlockSpec(memory_space=pl.ANY)
    out = pl.pallas_call(
        functools.partial(kernel, dims),
        out_shape=jax.ShapeDtypeStruct((tracers * levels * width, LANES), f32),
        in_specs=[hbm] * 10,
        out_specs=hbm,
        scratch_shapes=scratch,
        compiler_params=pltpu.CompilerParams(
            collective_id=0, has_side_effects=True, vmem_limit_bytes=63 * 2**20
        ),
        cost_estimate=pl.CostEstimate(flops=60_000_000, bytes_accessed=5_000_000, transcendentals=0),
        name="coupled_columns",
    )(
        state.reshape(tracers * levels * width, LANES),
        diffusion,
        vertical,
        coupling,
        land_sea,
        route_tile.reshape(route_src.shape),
        route_src,
        route_dst,
        pair_cols,
        intersection.reshape(intersection.shape[2:]),
    )
    return out.reshape(state.shape)


def solution(mesh):
    in_specs = (
        P("comp", None, None, "gx", "gy"),
        P("comp", "gx", "gy"),
        P("comp", None),
        P("comp", "gx", "gy"),
        P("comp", "gx", "gy"),
        P("comp", ("gx", "gy"), None, None),
        P("comp", ("gx", "gy"), None),
        P("comp", ("gx", "gy"), None),
        P("comp", ("gx", "gy"), None),
        P("comp", ("gx", "gy"), None, None, None),
    )
    out_specs = P("comp", None, None, "gx", "gy")
    run = functools.partial(body, mesh.shape["gx"], mesh.shape["gy"])
    return jax.shard_map(run, mesh=mesh, in_specs=in_specs, out_specs=out_specs, check_vma=False)
```

```python
import functools

import jax
import jax.numpy as jnp
from jax import lax
from jax.experimental import pallas as pl
from jax.experimental.pallas import tpu as pltpu
from jax.sharding import PartitionSpec as P

SUBSTEPS = 3
INTERVALS = 2
MESH = pl.DeviceIdType.MESH
HIGHEST = lax.Precision.HIGHEST
TOP = 8
SLAB = 8
LANES = 128
CHUNK = 4


def split_rows(value):
    first = value.astype(jnp.bfloat16)
    rest = value - first.astype(jnp.float32)
    second = rest.astype(jnp.bfloat16)
    third = (rest - second.astype(jnp.float32)).astype(jnp.bfloat16)
    return first, second, third


def pick(onehot, value):
    total = None
    for part in split_rows(value):
        term = jnp.dot(onehot, part, preferred_element_type=jnp.float32)
        total = term if total is None else total + term
    return total


def kernel(
    dims,
    state_ref,
    diff_hbm,
    mix_hbm,
    couple_hbm,
    sea_hbm,
    tile_hbm,
    src_hbm,
    dst_hbm,
    cols_hbm,
    weight_ref,
    out_hbm,
    state_v,
    weight_v,
    out_ref,
    diff_ref,
    mix_ref,
    couple_ref,
    sea_ref,
    tile_ref,
    src_ref,
    dst_ref,
    cols_ref,
    *rest,
):
    n_gx, n_gy, tiles, rows, pairs, tracers, levels, width = dims
    count = INTERVALS * SUBSTEPS
    groups = levels // SLAB
    per_row = LANES // (2 * width)
    pack_rows = -(-groups // per_row) * SLAB
    fields = rest[:count]
    rest = rest[count:]
    slabs = rest[: INTERVALS * (SUBSTEPS - 1)]
    rest = rest[INTERVALS * (SUBSTEPS - 1) :]
    pack_out = rest[: count * tracers]
    pack_in = rest[count * tracers : 2 * count * tracers]
    rest = rest[2 * count * tracers :]
    slab_count = INTERVALS * (SUBSTEPS - 1) + 1
    slab_out = rest[:slab_count]
    slab_in = rest[slab_count : 2 * slab_count]
    rest = rest[2 * slab_count :]
    sends = rest[:INTERVALS]
    recvs = rest[INTERVALS : 2 * INTERVALS]
    rest = rest[2 * INTERVALS :]
    (
        label_out,
        label_in,
        surf,
        contrib,
        gate_diff,
        gate_couple,
        gate_ref,
        mix_v,
        goal,
        onehot_v,
        dense_v,
        load_sem,
        halo_send,
        halo_recv,
        route_send,
        route_recv,
        out_sem,
    ) = rest

    comp = lax.axis_index("comp")
    gx = lax.axis_index("gx")
    gy = lax.axis_index("gy")
    other = 1 - comp
    mine = gx * n_gy + gy
    right = (comp, lax.rem(gx + 1, n_gx), gy)
    left = (comp, lax.rem(gx + n_gx - 1, n_gx), gy)
    across = (comp, gx, lax.rem(gy + 1, n_gy))

    loads = []
    for src, dst in (
        (tile_hbm, tile_ref),
        (dst_hbm, dst_ref),
        (state_ref, state_v),
        (sea_hbm, sea_ref),
        (diff_hbm, diff_ref),
        (couple_hbm, couple_ref),
        (mix_hbm, mix_ref),
        (src_hbm, src_ref),
        (cols_hbm, cols_ref),
        (weight_ref, weight_v),
    ):
        copy = pltpu.make_async_copy(src, dst, load_sem.at[len(loads)])
        copy.start()
        loads.append(copy)

    def peer(step):
        tile = lax.rem(mine + step, tiles)
        return tile, (other, tile // n_gy, lax.rem(tile, n_gy))

    barrier = pltpu.get_barrier_semaphore()
    for device in (right, left, across):
        pl.semaphore_signal(barrier, inc=1, device_id=device, device_id_type=MESH)

    def greet(step, carry):
        pl.semaphore_signal(barrier, inc=1, device_id=peer(step)[1], device_id_type=MESH)
        return carry

    lax.fori_loop(0, tiles, greet, 0)

    loads[0].wait()
    loads[1].wait()
    sub_ids = lax.broadcasted_iota(jnp.int32, (pairs, pairs), 0)
    lane_ids = lax.broadcasted_iota(jnp.int32, (pairs, pairs), 1)
    dest_row = tile_ref[0].astype(jnp.float32)
    dest_wide = jnp.broadcast_to(dest_row, (pairs, pairs))
    dest_col = jnp.sum(jnp.where(sub_ids == lane_ids, dest_wide, 0.0), axis=1, keepdims=True)
    same = dest_col == dest_wide
    rank_row = jnp.sum(jnp.where(same & (sub_ids < lane_ids), 1.0, 0.0), axis=0, keepdims=True)
    rank_col = jnp.sum(jnp.where(same & (lane_ids < sub_ids), 1.0, 0.0), axis=1, keepdims=True)
    place = (dest_row * rows + rank_row).astype(jnp.int32)
    slot_ids = lax.broadcasted_iota(jnp.int32, (tiles * rows, pairs), 0)
    onehot_v[...] = jnp.where(slot_ids == place, 1.0, 0.0).astype(jnp.bfloat16)
    tile_ids = lax.broadcasted_iota(jnp.int32, (tiles, pairs), 0).astype(jnp.float32)
    named = jnp.where(tile_ids == dest_row, (dst_ref[0] + 1).astype(jnp.float32), 0.0)
    slot_lane = lax.broadcasted_iota(jnp.int32, (pairs, LANES), 1).astype(jnp.float32)
    ranked = jnp.where(slot_lane == rank_col, 1.0, 0.0)
    label_out[...] = jnp.dot(
        named.astype(jnp.bfloat16), ranked.astype(jnp.bfloat16), preferred_element_type=jnp.float32
    ).reshape(tiles, 1, LANES)

    surf[...] = jnp.zeros(surf.shape, jnp.float32)

    def lane_of(height):
        return lax.broadcasted_iota(jnp.int32, (height, LANES), 1)

    pairs_lane = lane_of(SLAB) // 2

    def pack_tile(acc, value, j):
        return jnp.where(pairs_lane == j, pltpu.roll(value, 2 * j + 1, 1), acc)

    def unpack_tile(value, j):
        return pltpu.roll(value, LANES - 1 - 2 * j, 1)

    def pack_column(acc, value, x, skip):
        acc = list(acc)
        for g in range(skip, groups):
            part = value[(g - skip) * SLAB : (g - skip + 1) * SLAB]
            acc[g // per_row] = pack_tile(acc[g // per_row], part, (g % per_row) * width + x)
        return tuple(acc)

    def unpack_column(ref, x, skip):
        parts = []
        for g in range(skip, groups):
            low = (g // per_row) * SLAB
            parts.append(unpack_tile(ref[low : low + SLAB, :], (g % per_row) * width + x))
        return parts

    def exchange(number, to_right, to_left, packs):
        copies = []
        for i, (src, dst, device) in enumerate(
            ((packs[0], packs[1], across), (to_right[0], to_right[1], right), (to_left[0], to_left[1], left))
        ):
            copy = pltpu.make_async_remote_copy(
                src_ref=src,
                dst_ref=dst,
                send_sem=halo_send.at[number, i],
                recv_sem=halo_recv.at[number, i],
                device_id=device,
                device_id_type=MESH,
            )
            copy.start()
            copies.append(copy)
        return copies

    def x_sides(buf, f, low, high):
        span = pl.ds(low, high - low)
        to_right = (buf.at[f, width, span, :], buf.at[f, 0, span, :])
        to_left = (buf.at[f, 1, span, :], buf.at[f, width + 1, span, :])
        return to_right, to_left

    started = []
    numbers = iter(range(64))

    def send_halo(buf, f, low, high, out, into):
        copies = exchange(next(numbers), *x_sides(buf, f, low, high), (out, into))
        started.extend(copies)
        return copies

    def stencil(buf, f, x, low, height, turned):
        center = buf[f, x + 1, low : low + height]
        after = buf[f, x + 2, low : low + height]
        before = buf[f, x, low : low + height]
        above = buf[f, x + 1, low - 1 : low - 1 + height]
        below = buf[f, x + 1, low + 1 : low + 1 + height]
        lanes = lane_of(height)
        north = pltpu.roll(jnp.where(lanes == 0, turned, center), LANES - 1, 1)
        south = pltpu.roll(jnp.where(lanes == LANES - 1, turned, center), 1, 1)
        lap_h = (after + before) + (north + south) - 4.0 * center
        lap_v = (below + above) - 2.0 * center
        row = pl.ds(x, 1)
        gd = jnp.broadcast_to(gate_diff[row, :], (height, LANES))
        gv = jnp.broadcast_to(gate_ref[row, :], (height, LANES)) * mix_v[low - TOP : low - TOP + height]
        return center, center + (gd * lap_h + gv * lap_v)

    def with_ends(buf, f, x, value, height):
        buf[f, x + 1, TOP - 1 : TOP] = value[0:1]
        buf[f, x + 1, TOP + height : TOP + height + 1] = value[height - 1 : height]

    pl.semaphore_wait(barrier, tiles + 3)

    def post_all(source, target, number):
        def post(group, carry):
            for i in range(4):
                tile, device = peer(group * 4 + i)
                pltpu.make_async_remote_copy(
                    src_ref=source.at[tile],
                    dst_ref=target.at[mine],
                    send_sem=route_send.at[number],
                    recv_sem=route_recv.at[number],
                    device_id=device,
                    device_id_type=MESH,
                ).start()
            return carry

        lax.fori_loop(0, tiles // 4, post, 0)

    zero = jnp.zeros((SLAB, LANES), jnp.float32)
    empty = (zero,) * (pack_rows // SLAB)

    def store_pack(ref, acc):
        for i, part in enumerate(acc):
            ref[i * SLAB : (i + 1) * SLAB, :] = part

    loads[2].wait()
    pending = []
    for f in range(tracers):

        def load(chunk, acc):
            for i in range(CHUNK):
                x = chunk * CHUNK + i
                value = state_v[pl.ds(f * levels * width + x, levels, stride=width), :]
                fields[0][f, x + 1, TOP : TOP + levels] = value
                with_ends(fields[0], f, x, value, levels)
                surf[x, f : f + 1] = value[0:1]
                acc = pack_column(acc, value, x, 0)
            return acc

        store_pack(pack_out[f], lax.fori_loop(0, width // CHUNK, load, empty))
        pending.append(send_halo(fields[0], f, TOP, TOP + levels, pack_out[f], pack_in[f]))

    def remap(interval):
        lanes = lane_of(SLAB)

        def one(group, carry):
            for i in range(32):
                p = group * 32 + i
                left_side = surf[src_ref[0, 0, p]].astype(jnp.bfloat16)
                got = lax.dot_general(
                    left_side,
                    weight_v[p],
                    (((1,), (1,)), ((), ())),
                    preferred_element_type=jnp.float32,
                )
                got = jnp.where(lanes < cols_ref[0, 0, p], got, 0.0)
                contrib[pl.ds(pl.multiple_of(p * 8, 8), 8), :] = got
            return carry

        lax.fori_loop(0, pairs // 32, one, 0)
        onehot = onehot_v[...]
        for f in range(tracers):
            value = contrib[pl.ds(f, pairs, stride=8), :]
            sends[interval][:, :, f * LANES : (f + 1) * LANES] = pick(onehot, value).reshape(
                tiles, rows, LANES
            )
        post_all(sends[interval], recvs[interval], interval)

    def wait_whole(ref, sem):
        pltpu.make_async_copy(ref, ref, sem).wait()

    out_copies = []

    def write_out(f, low, high):
        span = pl.ds(f * levels * width + low * width, (high - low) * width)
        copy = pltpu.make_async_copy(
            out_ref.at[span, :], out_hbm.at[span, :], out_sem.at[len(out_copies)]
        )
        copy.start()
        out_copies.append(copy)

    for copy in loads[7:]:
        copy.wait()
    remap(0)
    post_all(label_out, label_in, INTERVALS)

    for copy in loads[3:7]:
        copy.wait()
    sea = sea_ref[0].astype(jnp.float32)
    gate = jnp.where(comp == 1, sea, jnp.ones_like(sea))
    gate_ref[...] = gate
    gate_diff[...] = gate * diff_ref[0]
    gate_couple[...] = gate * couple_ref[0]
    level_a = lax.broadcasted_iota(jnp.int32, (levels, levels), 0)
    level_b = lax.broadcasted_iota(jnp.int32, (levels, levels), 1)
    mix_col = jnp.sum(
        jnp.where(level_a == level_b, jnp.broadcast_to(mix_ref[...], (levels, levels)), 0.0),
        axis=1,
        keepdims=True,
    )
    mix_v[...] = jnp.broadcast_to(mix_col, (levels, LANES))

    inner = max(c for c in range(1, 9) if (width - 2) % c == 0)
    slab_number = 0
    slab_pending = []
    for interval in range(INTERVALS):
        final = interval == INTERVALS - 1
        first = interval * SUBSTEPS
        if interval > 0:
            remap(interval)

        def bulk_step(sub, f):
            buf = fields[first + sub]
            after = None if final and sub == SUBSTEPS - 1 else fields[first + sub + 1]
            pack = pack_in[(first + sub) * tracers + f]
            fresh = sub == 0 and interval > 0
            last = sub == SUBSTEPS - 1
            skip = 1 if last else 0
            low = TOP + skip * SLAB
            height = levels - skip * SLAB
            entry = slab_in[slab_number - 1] if fresh else None

            def column(x, acc):
                parts = unpack_column(pack, x, skip)
                if fresh:
                    parts[0] = unpack_tile(entry[...], f * width + x)
                turned = jnp.concatenate(parts, axis=0)
                _, value = stencil(buf, f, x, low, height, turned)
                if after is None:
                    start = f * levels * width + SLAB * width + x
                    out_ref[pl.ds(start, height, stride=width), :] = value
                    return acc
                after[f, x + 1, low : low + height] = value
                if last:
                    after[f, x + 1, TOP + levels : TOP + levels + 1] = value[height - 1 : height]
                else:
                    with_ends(after, f, x, value, height)
                return pack_column(acc, value, x, skip)

            def chunk(step, acc):
                for i in range(inner):
                    acc = column(1 + step * inner + i, acc)
                return acc

            copies = pending[f]
            copies[0].wait_recv()
            acc = lax.fori_loop(0, (width - 2) // inner, chunk, empty)
            copies[1].wait_recv()
            copies[2].wait_recv()
            acc = column(0, acc)
            acc = column(width - 1, acc)
            if after is None:
                write_out(f, SLAB, levels)
                return
            index = (first + sub + 1) * tracers + f
            store_pack(pack_out[index], acc)
            pending[f] = send_halo(after, f, low, low + height, pack_out[index], pack_in[index])

        def near_step(sub, number, waits):
            for copy in waits:
                copy.wait_recv()
            index = interval * (SUBSTEPS - 1) + sub - 1
            buf = fields[first] if sub == 0 else slabs[index]
            last = sub == SUBSTEPS - 1
            entry = None if sub == 0 and interval == 0 else slab_in[number - 1]
            after = None
            if not last:
                after = slabs[index + 1]
            elif not final:
                after = fields[first + SUBSTEPS]
            acc = zero
            for x in range(width):
                for f in range(tracers):
                    if entry is None:
                        turned = unpack_tile(pack_in[f][0:SLAB, :], x)
                    else:
                        turned = unpack_tile(entry[...], f * width + x)
                    center, value = stencil(buf, f, x, TOP, SLAB, turned)
                    force = jnp.broadcast_to(gate_couple[x : x + 1, :], (SLAB, LANES)) * (
                        jnp.broadcast_to(goal[f, x : x + 1, :], (SLAB, LANES)) - center
                    )
                    sub_row = lax.broadcasted_iota(jnp.int32, (SLAB, LANES), 0)
                    value = value + jnp.where(sub_row == 0, force, 0.0)
                    if after is None:
                        out_ref[pl.ds(f * levels * width + x, SLAB, stride=width), :] = value
                        continue
                    if last:
                        surf[x, f : f + 1] = value[0:1]
                    else:
                        after[f, x + 1, TOP + SLAB : TOP + SLAB + 1] = fields[first + sub + 1][
                            f, x + 1, TOP + SLAB : TOP + SLAB + 1
                        ]
                    after[f, x + 1, TOP : TOP + SLAB] = value
                    after[f, x + 1, TOP - 1 : TOP] = value[0:1]
                    acc = pack_tile(acc, value, f * width + x)
            if after is None:
                return []
            slab_out[number][...] = acc
            both = slice(None)
            return send_halo(after, both, TOP, TOP + SLAB, slab_out[number], slab_in[number])

        for copy in slab_pending:
            copy.wait_recv()
        slab_pending = []
        for f in range(tracers):
            bulk_step(0, f)

        if interval == 0:
            wait_whole(label_in, route_recv.at[INTERVALS])
            heard = label_in[...].reshape(tiles, LANES).astype(jnp.bfloat16)
            slots = tiles * rows
            spread_a = lax.broadcasted_iota(jnp.int32, (LANES, slots), 0)
            spread_b = lax.broadcasted_iota(jnp.int32, (LANES, slots), 1)
            spread = jnp.where(spread_a == spread_b % rows, 1.0, 0.0).astype(jnp.bfloat16)
            table = jnp.dot(heard, spread, preferred_element_type=jnp.float32)
            own_a = lax.broadcasted_iota(jnp.int32, (tiles, slots), 0)
            own_b = lax.broadcasted_iota(jnp.int32, (tiles, slots), 1)
            label_row = jnp.sum(jnp.where(own_a == own_b // rows, table, 0.0), axis=0, keepdims=True)
            block_ids = lax.broadcasted_iota(jnp.int32, (width, slots), 0) + 1
            dense_v[...] = jnp.where(block_ids.astype(jnp.float32) == label_row, 1.0, 0.0).astype(
                jnp.bfloat16
            )
        wait_whole(recvs[interval], route_recv.at[interval])
        dense = dense_v[...]
        for f in range(tracers):
            value = recvs[interval][:, :, f * LANES : (f + 1) * LANES].reshape(tiles * rows, LANES)
            goal[f] = sea * pick(dense, value)

        for sub in range(SUBSTEPS):
            slab_pending = near_step(sub, slab_number, slab_pending)
            if not (sub == SUBSTEPS - 1 and final):
                slab_number += 1
            if sub < SUBSTEPS - 1:
                for f in range(tracers):
                    bulk_step(sub + 1, f)

    for f in range(tracers):
        write_out(f, 0, SLAB)
    for copy in started:
        copy.wait_send()
    for interval in range(INTERVALS):
        wait_whole(sends[interval], route_send.at[interval])
    wait_whole(label_out, route_send.at[INTERVALS])
    for copy in out_copies:
        copy.wait()


def body(
    n_gx,
    n_gy,
    state,
    diffusion,
    vertical,
    coupling,
    land_sea,
    route_tile,
    route_src,
    route_dst,
    pair_cols,
    intersection,
):
    _, tracers, levels, width, lanes = state.shape
    assert lanes == LANES and n_gy == 2 and 2 * tracers * width <= LANES and n_gx % 2 == 0
    tiles = n_gx * n_gy
    pairs = route_src.shape[2]
    slots = max(2, 2 * pairs // tiles)
    rows = -(-slots // 8) * 8
    dims = (n_gx, n_gy, tiles, rows, pairs, tracers, levels, width)
    count = INTERVALS * SUBSTEPS
    slab_count = INTERVALS * (SUBSTEPS - 1) + 1
    f32 = jnp.float32
    groups = levels // SLAB
    pack_rows = -(-groups // (LANES // (2 * width))) * SLAB
    halos = count * tracers + slab_count
    scratch = [
        pltpu.VMEM((tracers * levels * width, LANES), f32),
        pltpu.VMEM(intersection.shape[2:], jnp.bfloat16),
        pltpu.VMEM((tracers * levels * width, LANES), f32),
        pltpu.VMEM(diffusion.shape, f32),
        pltpu.VMEM(vertical.shape, f32),
        pltpu.VMEM(coupling.shape, f32),
        pltpu.VMEM(land_sea.shape, jnp.int32),
        pltpu.VMEM(route_src.shape, jnp.int32),
        pltpu.SMEM(route_src.shape, jnp.int32),
        pltpu.VMEM(route_dst.shape, jnp.int32),
        pltpu.SMEM(pair_cols.shape, jnp.int32),
    ]
    scratch += [pltpu.VMEM((tracers, width + 2, TOP + levels + 8, LANES), f32)] * count
    scratch += [pltpu.VMEM((tracers, width + 2, TOP + SLAB + 8, LANES), f32)] * (
        INTERVALS * (SUBSTEPS - 1)
    )
    scratch += [pltpu.VMEM((pack_rows, LANES), f32)] * (2 * count * tracers)
    scratch += [pltpu.VMEM((SLAB, LANES), f32)] * (2 * slab_count)
    scratch += [pltpu.VMEM((tiles, rows, tracers * LANES), f32)] * (2 * INTERVALS)
    scratch += [
        pltpu.VMEM((tiles, 1, LANES), f32),
        pltpu.VMEM((tiles, 1, LANES), f32),
        pltpu.VMEM((width, 8, LANES), f32),
        pltpu.VMEM((pairs * 8, LANES), f32),
        pltpu.VMEM((width, LANES), f32),
        pltpu.VMEM((width, LANES), f32),
        pltpu.VMEM((width, LANES), f32),
        pltpu.VMEM((levels, LANES), f32),
        pltpu.VMEM((tracers, width, LANES), f32),
        pltpu.VMEM((tiles * rows, pairs), jnp.bfloat16),
        pltpu.VMEM((width, tiles * rows), jnp.bfloat16),
        pltpu.SemaphoreType.DMA((10,)),
        pltpu.SemaphoreType.DMA((halos, 3)),
        pltpu.SemaphoreType.DMA((halos, 3)),
        pltpu.SemaphoreType.DMA((INTERVALS + 1,)),
        pltpu.SemaphoreType.DMA((INTERVALS + 1,)),
        pltpu.SemaphoreType.DMA((2 * tracers,)),
    ]
    hbm = pl.BlockSpec(memory_space=pl.ANY)
    out = pl.pallas_call(
        functools.partial(kernel, dims),
        out_shape=jax.ShapeDtypeStruct((tracers * levels * width, LANES), f32),
        in_specs=[hbm] * 10,
        out_specs=hbm,
        scratch_shapes=scratch,
        compiler_params=pltpu.CompilerParams(
            collective_id=0, has_side_effects=True, vmem_limit_bytes=63 * 2**20
        ),
        cost_estimate=pl.CostEstimate(flops=60_000_000, bytes_accessed=5_000_000, transcendentals=0),
        name="coupled_columns",
    )(
        state.reshape(tracers * levels * width, LANES),
        diffusion,
        vertical,
        coupling,
        land_sea,
        route_tile.reshape(route_src.shape),
        route_src,
        route_dst,
        pair_cols,
        intersection.reshape(intersection.shape[2:]),
    )
    return out.reshape(state.shape)


def solution(mesh):
    in_specs = (
        P("comp", None, None, "gx", "gy"),
        P("comp", "gx", "gy"),
        P("comp", None),
        P("comp", "gx", "gy"),
        P("comp", "gx", "gy"),
        P("comp", ("gx", "gy"), None, None),
        P("comp", ("gx", "gy"), None),
        P("comp", ("gx", "gy"), None),
        P("comp", ("gx", "gy"), None),
        P("comp", ("gx", "gy"), None, None, None),
    )
    out_specs = P("comp", None, None, "gx", "gy")
    run = functools.partial(body, mesh.shape["gx"], mesh.shape["gy"])
    return jax.shard_map(run, mesh=mesh, in_specs=in_specs, out_specs=out_specs, check_vma=False)
```

```python
import functools

import jax
import jax.numpy as jnp
from jax import lax
from jax.experimental import pallas as pl
from jax.experimental.pallas import tpu as pltpu
from jax.sharding import PartitionSpec as P

SUBSTEPS = 3
INTERVALS = 2
MESH = pl.DeviceIdType.MESH
HIGHEST = lax.Precision.HIGHEST
TOP = 8
SLAB = 8
LANES = 128
CHUNK = 4


def split_rows(value):
    first = value.astype(jnp.bfloat16)
    rest = value - first.astype(jnp.float32)
    second = rest.astype(jnp.bfloat16)
    third = (rest - second.astype(jnp.float32)).astype(jnp.bfloat16)
    return first, second, third


def pick(onehot, value):
    total = None
    for part in split_rows(value):
        term = jnp.dot(onehot, part, preferred_element_type=jnp.float32)
        total = term if total is None else total + term
    return total


def kernel(
    dims,
    state_ref,
    diff_hbm,
    mix_hbm,
    couple_hbm,
    sea_hbm,
    tile_hbm,
    src_hbm,
    dst_hbm,
    cols_hbm,
    weight_ref,
    out_hbm,
    state_v,
    weight_v,
    out_ref,
    diff_ref,
    mix_ref,
    couple_ref,
    sea_ref,
    tile_ref,
    src_ref,
    dst_ref,
    cols_ref,
    *rest,
):
    n_gx, n_gy, tiles, rows, pairs, tracers, levels, width = dims
    count = INTERVALS * SUBSTEPS
    groups = levels // SLAB
    per_row = LANES // (2 * width)
    pack_rows = -(-groups // per_row) * SLAB
    fields = rest[:count]
    rest = rest[count:]
    slabs = rest[: INTERVALS * (SUBSTEPS - 1)]
    rest = rest[INTERVALS * (SUBSTEPS - 1) :]
    pack_out = rest[:count]
    pack_in = rest[count : 2 * count]
    rest = rest[2 * count :]
    slab_count = INTERVALS * (SUBSTEPS - 1) + 1
    slab_out = rest[:slab_count]
    slab_in = rest[slab_count : 2 * slab_count]
    rest = rest[2 * slab_count :]
    sends = rest[:INTERVALS]
    recvs = rest[INTERVALS : 2 * INTERVALS]
    rest = rest[2 * INTERVALS :]
    (
        label_out,
        label_in,
        surf,
        contrib,
        gate_diff,
        gate_couple,
        gate_ref,
        mix_v,
        goal,
        onehot_v,
        dense_v,
        load_sem,
        halo_send,
        halo_recv,
        route_send,
        route_recv,
        out_sem,
    ) = rest

    comp = lax.axis_index("comp")
    gx = lax.axis_index("gx")
    gy = lax.axis_index("gy")
    other = 1 - comp
    mine = gx * n_gy + gy
    right = (comp, lax.rem(gx + 1, n_gx), gy)
    left = (comp, lax.rem(gx + n_gx - 1, n_gx), gy)
    across = (comp, gx, lax.rem(gy + 1, n_gy))

    loads = []
    for src, dst in (
        (tile_hbm, tile_ref),
        (dst_hbm, dst_ref),
        (state_ref, state_v),
        (sea_hbm, sea_ref),
        (diff_hbm, diff_ref),
        (couple_hbm, couple_ref),
        (mix_hbm, mix_ref),
        (src_hbm, src_ref),
        (cols_hbm, cols_ref),
        (weight_ref, weight_v),
    ):
        copy = pltpu.make_async_copy(src, dst, load_sem.at[len(loads)])
        copy.start()
        loads.append(copy)

    def peer(step):
        tile = lax.rem(mine + step, tiles)
        return tile, (other, tile // n_gy, lax.rem(tile, n_gy))

    barrier = pltpu.get_barrier_semaphore()
    for device in (right, left, across):
        pl.semaphore_signal(barrier, inc=1, device_id=device, device_id_type=MESH)

    def greet(step, carry):
        pl.semaphore_signal(barrier, inc=1, device_id=peer(step)[1], device_id_type=MESH)
        return carry

    lax.fori_loop(0, tiles, greet, 0)

    loads[0].wait()
    loads[1].wait()
    sub_ids = lax.broadcasted_iota(jnp.int32, (pairs, pairs), 0)
    lane_ids = lax.broadcasted_iota(jnp.int32, (pairs, pairs), 1)
    dest_row = tile_ref[0].astype(jnp.float32)
    dest_wide = jnp.broadcast_to(dest_row, (pairs, pairs))
    dest_col = jnp.sum(jnp.where(sub_ids == lane_ids, dest_wide, 0.0), axis=1, keepdims=True)
    same = dest_col == dest_wide
    rank_row = jnp.sum(jnp.where(same & (sub_ids < lane_ids), 1.0, 0.0), axis=0, keepdims=True)
    rank_col = jnp.sum(jnp.where(same & (lane_ids < sub_ids), 1.0, 0.0), axis=1, keepdims=True)
    place = (dest_row * rows + rank_row).astype(jnp.int32)
    slot_ids = lax.broadcasted_iota(jnp.int32, (tiles * rows, pairs), 0)
    onehot_v[...] = jnp.where(slot_ids == place, 1.0, 0.0).astype(jnp.bfloat16)
    tile_ids = lax.broadcasted_iota(jnp.int32, (tiles, pairs), 0).astype(jnp.float32)
    named = jnp.where(tile_ids == dest_row, (dst_ref[0] + 1).astype(jnp.float32), 0.0)
    slot_lane = lax.broadcasted_iota(jnp.int32, (pairs, LANES), 1).astype(jnp.float32)
    ranked = jnp.where(slot_lane == rank_col, 1.0, 0.0)
    label_out[...] = jnp.dot(
        named.astype(jnp.bfloat16), ranked.astype(jnp.bfloat16), preferred_element_type=jnp.float32
    ).reshape(tiles, 1, LANES)

    surf[...] = jnp.zeros(surf.shape, jnp.float32)

    def lane_of(height):
        return lax.broadcasted_iota(jnp.int32, (height, LANES), 1)

    pairs_lane = lane_of(SLAB) // 2

    def pack_tile(acc, value, j):
        return jnp.where(pairs_lane == j, pltpu.roll(value, 2 * j + 1, 1), acc)

    def unpack_tile(value, j):
        return pltpu.roll(value, LANES - 1 - 2 * j, 1)

    def pack_column(acc, value, x, skip):
        acc = list(acc)
        for g in range(skip, groups):
            part = value[(g - skip) * SLAB : (g - skip + 1) * SLAB]
            acc[g // per_row] = pack_tile(acc[g // per_row], part, (g % per_row) * width + x)
        return tuple(acc)

    def unpack_column(ref, f, x, skip):
        parts = []
        for g in range(skip, groups):
            low = (g // per_row) * SLAB
            parts.append(unpack_tile(ref[f, low : low + SLAB, :], (g % per_row) * width + x))
        return parts

    def exchange(number, to_right, to_left, packs):
        copies = []
        for i, (src, dst, device) in enumerate(
            ((packs[0], packs[1], across), (to_right[0], to_right[1], right), (to_left[0], to_left[1], left))
        ):
            copy = pltpu.make_async_remote_copy(
                src_ref=src,
                dst_ref=dst,
                send_sem=halo_send.at[number, i],
                recv_sem=halo_recv.at[number, i],
                device_id=device,
                device_id_type=MESH,
            )
            copies.append(copy)
        return copies

    def x_sides(buf, f, low, high):
        span = pl.ds(low, high - low)
        to_right = (buf.at[f, width, span, :], buf.at[f, 0, span, :])
        to_left = (buf.at[f, 1, span, :], buf.at[f, width + 1, span, :])
        return to_right, to_left

    started = []

    def bulk_halo(n, f):
        low = TOP + (SLAB if n > 0 and n % SUBSTEPS == 0 else 0)
        sides = x_sides(fields[n], f, low, TOP + levels)
        return exchange(n * tracers + f, *sides, (pack_out[n].at[f], pack_in[n].at[f]))

    def slab_halo(number, buf):
        sides = x_sides(buf, slice(None), TOP, TOP + SLAB)
        copies = exchange(count * tracers + number, *sides, (slab_out[number], slab_in[number]))
        for copy in copies:
            copy.start()
        started.extend(copies)
        return copies

    def stencil(buf, f, x, low, height, turned):
        center = buf[f, x + 1, low : low + height]
        after = buf[f, x + 2, low : low + height]
        before = buf[f, x, low : low + height]
        above = buf[f, x + 1, low - 1 : low - 1 + height]
        below = buf[f, x + 1, low + 1 : low + 1 + height]
        lanes = lane_of(height)
        north = pltpu.roll(jnp.where(lanes == 0, turned, center), LANES - 1, 1)
        south = pltpu.roll(jnp.where(lanes == LANES - 1, turned, center), 1, 1)
        lap_h = (after + before) + (north + south) - 4.0 * center
        lap_v = (below + above) - 2.0 * center
        row = pl.ds(x, 1)
        gd = jnp.broadcast_to(gate_diff[row, :], (height, LANES))
        gv = jnp.broadcast_to(gate_ref[row, :], (height, LANES)) * mix_v[low - TOP : low - TOP + height]
        return center, center + (gd * lap_h + gv * lap_v)

    def with_ends(buf, f, x, value, height):
        buf[f, x + 1, TOP - 1 : TOP] = value[0:1]
        buf[f, x + 1, TOP + height : TOP + height + 1] = value[height - 1 : height]

    def post_all(source, target, number):
        def post(group, carry):
            for i in range(4):
                tile, device = peer(group * 4 + i)
                pltpu.make_async_remote_copy(
                    src_ref=source.at[tile],
                    dst_ref=target.at[mine],
                    send_sem=route_send.at[number],
                    recv_sem=route_recv.at[number],
                    device_id=device,
                    device_id_type=MESH,
                ).start()
            return carry

        lax.fori_loop(0, tiles // 4, post, 0)

    zero = jnp.zeros((SLAB, LANES), jnp.float32)
    empty = (zero,) * (pack_rows // SLAB)

    def store_pack(ref, f, acc):
        for i, part in enumerate(acc):
            ref[f, i * SLAB : (i + 1) * SLAB, :] = part

    loads[2].wait()
    for f in range(tracers):

        def load(chunk, acc):
            for i in range(CHUNK):
                x = chunk * CHUNK + i
                value = state_v[pl.ds(f * levels * width + x, levels, stride=width), :]
                fields[0][f, x + 1, TOP : TOP + levels] = value
                with_ends(fields[0], f, x, value, levels)
                surf[x, f : f + 1] = value[0:1]
                acc = pack_column(acc, value, x, 0)
            return acc

        store_pack(pack_out[0], f, lax.fori_loop(0, width // CHUNK, load, empty))

    def remap(interval):
        lanes = lane_of(SLAB)

        def one(group, carry):
            for i in range(32):
                p = group * 32 + i
                left_side = surf[src_ref[0, 0, p]].astype(jnp.bfloat16)
                got = lax.dot_general(
                    left_side,
                    weight_v[p],
                    (((1,), (1,)), ((), ())),
                    preferred_element_type=jnp.float32,
                )
                got = jnp.where(lanes < cols_ref[0, 0, p], got, 0.0)
                contrib[pl.ds(pl.multiple_of(p * 8, 8), 8), :] = got
            return carry

        lax.fori_loop(0, pairs // 32, one, 0)
        onehot = onehot_v[...]
        for f in range(tracers):
            value = contrib[pl.ds(f, pairs, stride=8), :]
            sends[interval][:, :, f * LANES : (f + 1) * LANES] = pick(onehot, value).reshape(
                tiles, rows, LANES
            )

    def wait_whole(ref, sem):
        pltpu.make_async_copy(ref, ref, sem).wait()

    def out_copy(f, low, high, number):
        begin = pl.multiple_of(f * levels * width + low * width, 8)
        span = pl.ds(begin, (high - low) * width)
        return pltpu.make_async_copy(
            out_ref.at[span, :], out_hbm.at[span, :], out_sem.at[number * tracers + f]
        )

    for copy in loads[7:]:
        copy.wait()
    remap(0)
    pl.semaphore_wait(barrier, tiles + 3)
    for f in range(tracers):
        for copy in bulk_halo(0, f):
            copy.start()
    post_all(sends[0], recvs[0], 0)
    post_all(label_out, label_in, INTERVALS)

    for copy in loads[3:7]:
        copy.wait()
    sea = sea_ref[0].astype(jnp.float32)
    gate = jnp.where(comp == 1, sea, jnp.ones_like(sea))
    gate_ref[...] = gate
    gate_diff[...] = gate * diff_ref[0]
    gate_couple[...] = gate * couple_ref[0]
    level_a = lax.broadcasted_iota(jnp.int32, (levels, levels), 0)
    level_b = lax.broadcasted_iota(jnp.int32, (levels, levels), 1)
    mix_col = jnp.sum(
        jnp.where(level_a == level_b, jnp.broadcast_to(mix_ref[...], (levels, levels)), 0.0),
        axis=1,
        keepdims=True,
    )
    mix_v[...] = jnp.broadcast_to(mix_col, (levels, LANES))

    inner = max(c for c in range(1, 9) if (width - 2) % c == 0)
    slab_number = 0
    slab_pending = []
    for interval in range(INTERVALS):
        final = interval == INTERVALS - 1
        first = interval * SUBSTEPS
        if interval > 0:
            remap(interval)
            post_all(sends[interval], recvs[interval], interval)

        def bulk_step(sub):
            n = first + sub
            buf = fields[n]
            last = sub == SUBSTEPS - 1
            after = None if final and last else fields[n + 1]
            fresh = sub == 0 and interval > 0
            skip = 1 if last else 0
            low = TOP + skip * SLAB
            height = levels - skip * SLAB
            entry = slab_in[slab_number - 1] if fresh else None

            def per_tracer(f, carry):
                def column(x, acc):
                    parts = unpack_column(pack_in[n], f, x, skip)
                    if fresh:
                        parts[0] = unpack_tile(entry[...], f * width + x)
                    turned = jnp.concatenate(parts, axis=0)
                    _, value = stencil(buf, f, x, low, height, turned)
                    if after is None:
                        start = f * levels * width + SLAB * width + x
                        out_ref[pl.ds(start, height, stride=width), :] = value
                        return acc
                    after[f, x + 1, low : low + height] = value
                    if last:
                        after[f, x + 1, TOP + levels : TOP + levels + 1] = value[height - 1 : height]
                    else:
                        with_ends(after, f, x, value, height)
                    return pack_column(acc, value, x, skip)

                def chunk(step, acc):
                    for i in range(inner):
                        acc = column(1 + step * inner + i, acc)
                    return acc

                copies = bulk_halo(n, f)
                copies[0].wait_recv()
                acc = lax.fori_loop(0, (width - 2) // inner, chunk, empty)
                copies[1].wait_recv()
                copies[2].wait_recv()
                acc = column(0, acc)
                acc = column(width - 1, acc)
                if after is None:
                    out_copy(f, SLAB, levels, 0).start()
                    return carry
                store_pack(pack_out[n + 1], f, acc)
                for copy in bulk_halo(n + 1, f):
                    copy.start()
                return carry

            lax.fori_loop(0, tracers, per_tracer, 0)

        def near_step(sub, number, waits):
            for copy in waits:
                copy.wait_recv()
            index = interval * (SUBSTEPS - 1) + sub - 1
            buf = fields[first] if sub == 0 else slabs[index]
            last = sub == SUBSTEPS - 1
            entry = None if sub == 0 and interval == 0 else slab_in[number - 1]
            after = None
            if not last:
                after = slabs[index + 1]
            elif not final:
                after = fields[first + SUBSTEPS]
            acc = zero
            for x in range(width):
                for f in range(tracers):
                    if entry is None:
                        turned = unpack_tile(pack_in[0][f, 0:SLAB, :], x)
                    else:
                        turned = unpack_tile(entry[...], f * width + x)
                    center, value = stencil(buf, f, x, TOP, SLAB, turned)
                    force = jnp.broadcast_to(gate_couple[x : x + 1, :], (SLAB, LANES)) * (
                        jnp.broadcast_to(goal[f, x : x + 1, :], (SLAB, LANES)) - center
                    )
                    sub_row = lax.broadcasted_iota(jnp.int32, (SLAB, LANES), 0)
                    value = value + jnp.where(sub_row == 0, force, 0.0)
                    if after is None:
                        out_ref[pl.ds(f * levels * width + x, SLAB, stride=width), :] = value
                        continue
                    if last:
                        surf[x, f : f + 1] = value[0:1]
                    else:
                        after[f, x + 1, TOP + SLAB : TOP + SLAB + 1] = fields[first + sub + 1][
                            f, x + 1, TOP + SLAB : TOP + SLAB + 1
                        ]
                    after[f, x + 1, TOP : TOP + SLAB] = value
                    after[f, x + 1, TOP - 1 : TOP] = value[0:1]
                    acc = pack_tile(acc, value, f * width + x)
            if after is None:
                return []
            slab_out[number][...] = acc
            return slab_halo(number, after)

        for copy in slab_pending:
            copy.wait_recv()
        slab_pending = []
        bulk_step(0)

        if interval == 0:
            wait_whole(label_in, route_recv.at[INTERVALS])
            heard = label_in[...].reshape(tiles, LANES).astype(jnp.bfloat16)
            slots = tiles * rows
            spread_a = lax.broadcasted_iota(jnp.int32, (LANES, slots), 0)
            spread_b = lax.broadcasted_iota(jnp.int32, (LANES, slots), 1)
            spread = jnp.where(spread_a == spread_b % rows, 1.0, 0.0).astype(jnp.bfloat16)
            table = jnp.dot(heard, spread, preferred_element_type=jnp.float32)
            own_a = lax.broadcasted_iota(jnp.int32, (tiles, slots), 0)
            own_b = lax.broadcasted_iota(jnp.int32, (tiles, slots), 1)
            label_row = jnp.sum(jnp.where(own_a == own_b // rows, table, 0.0), axis=0, keepdims=True)
            block_ids = lax.broadcasted_iota(jnp.int32, (width, slots), 0) + 1
            dense_v[...] = jnp.where(block_ids.astype(jnp.float32) == label_row, 1.0, 0.0).astype(
                jnp.bfloat16
            )
        wait_whole(recvs[interval], route_recv.at[interval])
        dense = dense_v[...]
        for f in range(tracers):
            value = recvs[interval][:, :, f * LANES : (f + 1) * LANES].reshape(tiles * rows, LANES)
            goal[f] = sea * pick(dense, value)

        for sub in range(SUBSTEPS):
            slab_pending = near_step(sub, slab_number, slab_pending)
            if not (sub == SUBSTEPS - 1 and final):
                slab_number += 1
            if sub < SUBSTEPS - 1:
                bulk_step(sub + 1)

    for f in range(tracers):
        out_copy(f, 0, SLAB, 1).start()
    for copy in started:
        copy.wait_send()
    for n in range(count):
        for f in range(tracers):
            for copy in bulk_halo(n, f):
                copy.wait_send()
    for interval in range(INTERVALS):
        wait_whole(sends[interval], route_send.at[interval])
    wait_whole(label_out, route_send.at[INTERVALS])
    for f in range(tracers):
        out_copy(f, SLAB, levels, 0).wait()
        out_copy(f, 0, SLAB, 1).wait()


def body(
    n_gx,
    n_gy,
    state,
    diffusion,
    vertical,
    coupling,
    land_sea,
    route_tile,
    route_src,
    route_dst,
    pair_cols,
    intersection,
):
    _, tracers, levels, width, lanes = state.shape
    assert lanes == LANES and n_gy == 2 and 2 * tracers * width <= LANES and n_gx % 2 == 0
    tiles = n_gx * n_gy
    pairs = route_src.shape[2]
    slots = max(2, 2 * pairs // tiles)
    rows = -(-slots // 8) * 8
    dims = (n_gx, n_gy, tiles, rows, pairs, tracers, levels, width)
    count = INTERVALS * SUBSTEPS
    slab_count = INTERVALS * (SUBSTEPS - 1) + 1
    f32 = jnp.float32
    groups = levels // SLAB
    pack_rows = -(-groups // (LANES // (2 * width))) * SLAB
    halos = count * tracers + slab_count
    scratch = [
        pltpu.VMEM((tracers * levels * width, LANES), f32),
        pltpu.VMEM(intersection.shape[2:], jnp.bfloat16),
        pltpu.VMEM((tracers * levels * width, LANES), f32),
        pltpu.VMEM(diffusion.shape, f32),
        pltpu.VMEM(vertical.shape, f32),
        pltpu.VMEM(coupling.shape, f32),
        pltpu.VMEM(land_sea.shape, jnp.int32),
        pltpu.VMEM(route_src.shape, jnp.int32),
        pltpu.SMEM(route_src.shape, jnp.int32),
        pltpu.VMEM(route_dst.shape, jnp.int32),
        pltpu.SMEM(pair_cols.shape, jnp.int32),
    ]
    scratch += [pltpu.VMEM((tracers, width + 2, TOP + levels + 8, LANES), f32)] * count
    scratch += [pltpu.VMEM((tracers, width + 2, TOP + SLAB + 8, LANES), f32)] * (
        INTERVALS * (SUBSTEPS - 1)
    )
    scratch += [pltpu.VMEM((tracers, pack_rows, LANES), f32)] * (2 * count)
    scratch += [pltpu.VMEM((SLAB, LANES), f32)] * (2 * slab_count)
    scratch += [pltpu.VMEM((tiles, rows, tracers * LANES), f32)] * (2 * INTERVALS)
    scratch += [
        pltpu.VMEM((tiles, 1, LANES), f32),
        pltpu.VMEM((tiles, 1, LANES), f32),
        pltpu.VMEM((width, 8, LANES), f32),
        pltpu.VMEM((pairs * 8, LANES), f32),
        pltpu.VMEM((width, LANES), f32),
        pltpu.VMEM((width, LANES), f32),
        pltpu.VMEM((width, LANES), f32),
        pltpu.VMEM((levels, LANES), f32),
        pltpu.VMEM((tracers, width, LANES), f32),
        pltpu.VMEM((tiles * rows, pairs), jnp.bfloat16),
        pltpu.VMEM((width, tiles * rows), jnp.bfloat16),
        pltpu.SemaphoreType.DMA((10,)),
        pltpu.SemaphoreType.DMA((halos, 3)),
        pltpu.SemaphoreType.DMA((halos, 3)),
        pltpu.SemaphoreType.DMA((INTERVALS + 1,)),
        pltpu.SemaphoreType.DMA((INTERVALS + 1,)),
        pltpu.SemaphoreType.DMA((2 * tracers,)),
    ]
    hbm = pl.BlockSpec(memory_space=pl.ANY)
    out = pl.pallas_call(
        functools.partial(kernel, dims),
        out_shape=jax.ShapeDtypeStruct((tracers * levels * width, LANES), f32),
        in_specs=[hbm] * 10,
        out_specs=hbm,
        scratch_shapes=scratch,
        compiler_params=pltpu.CompilerParams(
            collective_id=0, has_side_effects=True, vmem_limit_bytes=63 * 2**20
        ),
        cost_estimate=pl.CostEstimate(flops=60_000_000, bytes_accessed=5_000_000, transcendentals=0),
        name="coupled_columns",
    )(
        state.reshape(tracers * levels * width, LANES),
        diffusion,
        vertical,
        coupling,
        land_sea,
        route_tile.reshape(route_src.shape),
        route_src,
        route_dst,
        pair_cols,
        intersection.reshape(intersection.shape[2:]),
    )
    return out.reshape(state.shape)


def solution(mesh):
    in_specs = (
        P("comp", None, None, "gx", "gy"),
        P("comp", "gx", "gy"),
        P("comp", None),
        P("comp", "gx", "gy"),
        P("comp", "gx", "gy"),
        P("comp", ("gx", "gy"), None, None),
        P("comp", ("gx", "gy"), None),
        P("comp", ("gx", "gy"), None),
        P("comp", ("gx", "gy"), None),
        P("comp", ("gx", "gy"), None, None, None),
    )
    out_specs = P("comp", None, None, "gx", "gy")
    run = functools.partial(body, mesh.shape["gx"], mesh.shape["gy"])
    return jax.shard_map(run, mesh=mesh, in_specs=in_specs, out_specs=out_specs, check_vma=False)
```

```python
import functools

import jax
import jax.numpy as jnp
from jax import lax
from jax.experimental import pallas as pl
from jax.experimental.pallas import tpu as pltpu
from jax.sharding import PartitionSpec as P

SUBSTEPS = 3
INTERVALS = 2
MESH = pl.DeviceIdType.MESH
HIGHEST = lax.Precision.HIGHEST
TOP = 8
SLAB = 8
LANES = 128
CHUNK = 4


def split_rows(value):
    first = value.astype(jnp.bfloat16)
    rest = value - first.astype(jnp.float32)
    second = rest.astype(jnp.bfloat16)
    third = (rest - second.astype(jnp.float32)).astype(jnp.bfloat16)
    return first, second, third


def pick(onehot, value):
    total = None
    for part in split_rows(value):
        term = jnp.dot(onehot, part, preferred_element_type=jnp.float32)
        total = term if total is None else total + term
    return total


def kernel(
    dims,
    state_ref,
    diff_hbm,
    mix_hbm,
    couple_hbm,
    sea_hbm,
    tile_hbm,
    src_hbm,
    dst_hbm,
    cols_hbm,
    weight_ref,
    out_hbm,
    state_v,
    weight_v,
    out_ref,
    diff_ref,
    mix_ref,
    couple_ref,
    sea_ref,
    tile_ref,
    src_ref,
    dst_ref,
    cols_ref,
    *rest,
):
    n_gx, n_gy, tiles, rows, pairs, tracers, levels, width = dims
    count = INTERVALS * SUBSTEPS
    groups = levels // SLAB
    per_row = LANES // (2 * width)
    pack_rows = -(-groups // per_row) * SLAB
    fields = rest[:count]
    rest = rest[count:]
    slabs = rest[: INTERVALS * (SUBSTEPS - 1)]
    rest = rest[INTERVALS * (SUBSTEPS - 1) :]
    pack_out = rest[:count]
    pack_in = rest[count : 2 * count]
    rest = rest[2 * count :]
    slab_count = INTERVALS * (SUBSTEPS - 1) + 1
    slab_out = rest[:slab_count]
    slab_in = rest[slab_count : 2 * slab_count]
    rest = rest[2 * slab_count :]
    sends = rest[:INTERVALS]
    recvs = rest[INTERVALS : 2 * INTERVALS]
    rest = rest[2 * INTERVALS :]
    (
        label_out,
        label_in,
        surf,
        contrib,
        gate_diff,
        gate_couple,
        gate_ref,
        mix_v,
        goal,
        onehot_v,
        dense_v,
        load_sem,
        halo_send,
        halo_recv,
        route_send,
        route_recv,
        out_sem,
    ) = rest

    comp = lax.axis_index("comp")
    gx = lax.axis_index("gx")
    gy = lax.axis_index("gy")
    other = 1 - comp
    mine = gx * n_gy + gy
    right = (comp, lax.rem(gx + 1, n_gx), gy)
    left = (comp, lax.rem(gx + n_gx - 1, n_gx), gy)
    across = (comp, gx, lax.rem(gy + 1, n_gy))

    loads = []
    for src, dst in (
        (tile_hbm, tile_ref),
        (dst_hbm, dst_ref),
        (state_ref, state_v),
        (sea_hbm, sea_ref),
        (diff_hbm, diff_ref),
        (couple_hbm, couple_ref),
        (mix_hbm, mix_ref),
        (src_hbm, src_ref),
        (cols_hbm, cols_ref),
        (weight_ref, weight_v),
    ):
        copy = pltpu.make_async_copy(src, dst, load_sem.at[len(loads)])
        copy.start()
        loads.append(copy)

    def peer(step):
        tile = lax.rem(mine + step, tiles)
        return tile, (other, tile // n_gy, lax.rem(tile, n_gy))

    barrier = pltpu.get_barrier_semaphore()
    for device in (right, left, across):
        pl.semaphore_signal(barrier, inc=1, device_id=device, device_id_type=MESH)

    def greet(step, carry):
        pl.semaphore_signal(barrier, inc=1, device_id=peer(step)[1], device_id_type=MESH)
        return carry

    lax.fori_loop(0, tiles, greet, 0)

    loads[0].wait()
    loads[1].wait()
    sub_ids = lax.broadcasted_iota(jnp.int32, (pairs, pairs), 0)
    lane_ids = lax.broadcasted_iota(jnp.int32, (pairs, pairs), 1)
    dest_row = tile_ref[0].astype(jnp.float32)
    dest_wide = jnp.broadcast_to(dest_row, (pairs, pairs))
    dest_col = jnp.sum(jnp.where(sub_ids == lane_ids, dest_wide, 0.0), axis=1, keepdims=True)
    same = dest_col == dest_wide
    rank_row = jnp.sum(jnp.where(same & (sub_ids < lane_ids), 1.0, 0.0), axis=0, keepdims=True)
    rank_col = jnp.sum(jnp.where(same & (lane_ids < sub_ids), 1.0, 0.0), axis=1, keepdims=True)
    place = (dest_row * rows + rank_row).astype(jnp.int32)
    slot_ids = lax.broadcasted_iota(jnp.int32, (tiles * rows, pairs), 0)
    onehot_v[...] = jnp.where(slot_ids == place, 1.0, 0.0).astype(jnp.bfloat16)
    tile_ids = lax.broadcasted_iota(jnp.int32, (tiles, pairs), 0).astype(jnp.float32)
    named = jnp.where(tile_ids == dest_row, (dst_ref[0] + 1).astype(jnp.float32), 0.0)
    slot_lane = lax.broadcasted_iota(jnp.int32, (pairs, LANES), 1).astype(jnp.float32)
    ranked = jnp.where(slot_lane == rank_col, 1.0, 0.0)
    label_out[...] = jnp.dot(
        named.astype(jnp.bfloat16), ranked.astype(jnp.bfloat16), preferred_element_type=jnp.float32
    ).reshape(tiles, 1, LANES)

    surf[...] = jnp.zeros(surf.shape, jnp.float32)

    def lane_of(height):
        return lax.broadcasted_iota(jnp.int32, (height, LANES), 1)

    pairs_lane = lane_of(SLAB) // 2

    def pack_tile(acc, value, j):
        return jnp.where(pairs_lane == j, pltpu.roll(value, 2 * j + 1, 1), acc)

    def unpack_tile(value, j):
        return pltpu.roll(value, LANES - 1 - 2 * j, 1)

    def pack_column(acc, value, x, skip):
        acc = list(acc)
        for g in range(skip, groups):
            part = value[(g - skip) * SLAB : (g - skip + 1) * SLAB]
            acc[g // per_row] = pack_tile(acc[g // per_row], part, (g % per_row) * width + x)
        return tuple(acc)

    def unpack_column(ref, f, x, skip):
        parts = []
        for g in range(skip, groups):
            low = (g // per_row) * SLAB
            parts.append(unpack_tile(ref[f, low : low + SLAB, :], (g % per_row) * width + x))
        return parts

    def exchange(number, to_right, to_left, packs):
        copies = []
        for i, (src, dst, device) in enumerate(
            ((packs[0], packs[1], across), (to_right[0], to_right[1], right), (to_left[0], to_left[1], left))
        ):
            copy = pltpu.make_async_remote_copy(
                src_ref=src,
                dst_ref=dst,
                send_sem=halo_send.at[number, i],
                recv_sem=halo_recv.at[number, i],
                device_id=device,
                device_id_type=MESH,
            )
            copies.append(copy)
        return copies

    def x_sides(buf, f, low, high):
        span = pl.ds(low, high - low)
        to_right = (buf.at[f, width, span, :], buf.at[f, 0, span, :])
        to_left = (buf.at[f, 1, span, :], buf.at[f, width + 1, span, :])
        return to_right, to_left

    started = []

    def bulk_halo(n, f):
        low = TOP + (SLAB if n > 0 and n % SUBSTEPS == 0 else 0)
        sides = x_sides(fields[n], f, low, TOP + levels)
        return exchange(n * tracers + f, *sides, (pack_out[n].at[f], pack_in[n].at[f]))

    def slab_halo(number, buf):
        sides = x_sides(buf, slice(None), TOP, TOP + SLAB)
        copies = exchange(count * tracers + number, *sides, (slab_out[number], slab_in[number]))
        for copy in copies:
            copy.start()
        started.extend(copies)
        return copies

    def stencil(buf, f, x, low, height, turned):
        center = buf[f, x + 1, low : low + height]
        after = buf[f, x + 2, low : low + height]
        before = buf[f, x, low : low + height]
        above = buf[f, x + 1, low - 1 : low - 1 + height]
        below = buf[f, x + 1, low + 1 : low + 1 + height]
        lanes = lane_of(height)
        north = pltpu.roll(jnp.where(lanes == 0, turned, center), LANES - 1, 1)
        south = pltpu.roll(jnp.where(lanes == LANES - 1, turned, center), 1, 1)
        lap_h = (after + before) + (north + south) - 4.0 * center
        lap_v = (below + above) - 2.0 * center
        row = pl.ds(x, 1)
        gd = jnp.broadcast_to(gate_diff[row, :], (height, LANES))
        gv = jnp.broadcast_to(gate_ref[row, :], (height, LANES)) * mix_v[low - TOP : low - TOP + height]
        return center, center + (gd * lap_h + gv * lap_v)

    def with_ends(buf, f, x, value, height):
        buf[f, x + 1, TOP - 1 : TOP] = value[0:1]
        buf[f, x + 1, TOP + height : TOP + height + 1] = value[height - 1 : height]

    def post_all(source, target, number):
        def post(group, carry):
            for i in range(4):
                tile, device = peer(group * 4 + i)
                pltpu.make_async_remote_copy(
                    src_ref=source.at[tile],
                    dst_ref=target.at[mine],
                    send_sem=route_send.at[number],
                    recv_sem=route_recv.at[number],
                    device_id=device,
                    device_id_type=MESH,
                ).start()
            return carry

        lax.fori_loop(0, tiles // 4, post, 0)

    zero = jnp.zeros((SLAB, LANES), jnp.float32)
    empty = (zero,) * (pack_rows // SLAB)

    def store_pack(ref, f, acc):
        for i, part in enumerate(acc):
            ref[f, i * SLAB : (i + 1) * SLAB, :] = part

    loads[2].wait()
    for f in range(tracers):

        def load(chunk, acc):
            for i in range(CHUNK):
                x = chunk * CHUNK + i
                value = state_v[pl.ds(f * levels * width + x, levels, stride=width), :]
                fields[0][f, x + 1, TOP : TOP + levels] = value
                with_ends(fields[0], f, x, value, levels)
                surf[x, f : f + 1] = value[0:1]
                acc = pack_column(acc, value, x, 0)
            return acc

        store_pack(pack_out[0], f, lax.fori_loop(0, width // CHUNK, load, empty))

    def remap(interval):
        lanes = lane_of(SLAB)

        def one(group, carry):
            for i in range(32):
                p = group * 32 + i
                left_side = surf[src_ref[0, 0, p]].astype(jnp.bfloat16)
                got = lax.dot_general(
                    left_side,
                    weight_v[p],
                    (((1,), (1,)), ((), ())),
                    preferred_element_type=jnp.float32,
                )
                got = jnp.where(lanes < cols_ref[0, 0, p], got, 0.0)
                contrib[pl.ds(pl.multiple_of(p * 8, 8), 8), :] = got
            return carry

        lax.fori_loop(0, pairs // 32, one, 0)
        onehot = onehot_v[...]
        for f in range(tracers):
            value = contrib[pl.ds(f, pairs, stride=8), :]
            sends[interval][:, :, f * LANES : (f + 1) * LANES] = pick(onehot, value).reshape(
                tiles, rows, LANES
            )

    def wait_whole(ref, sem):
        pltpu.make_async_copy(ref, ref, sem).wait()

    def out_copy(f, low, high, number):
        span = pl.ds(low, high - low)
        return pltpu.make_async_copy(
            out_ref.at[f, :, span, :], out_hbm.at[f, :, span, :], out_sem.at[number * tracers + f]
        )

    for copy in loads[7:]:
        copy.wait()
    remap(0)
    pl.semaphore_wait(barrier, tiles + 3)
    for f in range(tracers):
        for copy in bulk_halo(0, f):
            copy.start()
    post_all(sends[0], recvs[0], 0)
    post_all(label_out, label_in, INTERVALS)

    for copy in loads[3:7]:
        copy.wait()
    sea = sea_ref[0].astype(jnp.float32)
    gate = jnp.where(comp == 1, sea, jnp.ones_like(sea))
    gate_ref[...] = gate
    gate_diff[...] = gate * diff_ref[0]
    gate_couple[...] = gate * couple_ref[0]
    level_a = lax.broadcasted_iota(jnp.int32, (levels, levels), 0)
    level_b = lax.broadcasted_iota(jnp.int32, (levels, levels), 1)
    mix_col = jnp.sum(
        jnp.where(level_a == level_b, jnp.broadcast_to(mix_ref[...], (levels, levels)), 0.0),
        axis=1,
        keepdims=True,
    )
    mix_v[...] = jnp.broadcast_to(mix_col, (levels, LANES))

    inner = max(c for c in range(1, 9) if (width - 2) % c == 0)
    slab_number = 0
    slab_pending = []
    for interval in range(INTERVALS):
        final = interval == INTERVALS - 1
        first = interval * SUBSTEPS
        if interval > 0:
            remap(interval)
            post_all(sends[interval], recvs[interval], interval)

        def bulk_step(sub):
            n = first + sub
            buf = fields[n]
            last = sub == SUBSTEPS - 1
            after = None if final and last else fields[n + 1]
            fresh = sub == 0 and interval > 0
            skip = 1 if last else 0
            low = TOP + skip * SLAB
            height = levels - skip * SLAB
            entry = slab_in[slab_number - 1] if fresh else None

            def per_tracer(f, carry):
                def column(x, acc):
                    parts = unpack_column(pack_in[n], f, x, skip)
                    if fresh:
                        parts[0] = unpack_tile(entry[...], f * width + x)
                    turned = jnp.concatenate(parts, axis=0)
                    _, value = stencil(buf, f, x, low, height, turned)
                    if after is None:
                        out_ref[f, x, SLAB:levels] = value
                        return acc
                    after[f, x + 1, low : low + height] = value
                    if last:
                        after[f, x + 1, TOP + levels : TOP + levels + 1] = value[height - 1 : height]
                    else:
                        with_ends(after, f, x, value, height)
                    return pack_column(acc, value, x, skip)

                def chunk(step, acc):
                    for i in range(inner):
                        acc = column(1 + step * inner + i, acc)
                    return acc

                copies = bulk_halo(n, f)
                copies[0].wait_recv()
                acc = lax.fori_loop(0, (width - 2) // inner, chunk, empty)
                copies[1].wait_recv()
                copies[2].wait_recv()
                acc = column(0, acc)
                acc = column(width - 1, acc)
                if after is None:
                    out_copy(f, SLAB, levels, 0).start()
                    return carry
                store_pack(pack_out[n + 1], f, acc)
                for copy in bulk_halo(n + 1, f):
                    copy.start()
                return carry

            lax.fori_loop(0, tracers, per_tracer, 0)

        def near_step(sub, number, waits):
            for copy in waits:
                copy.wait_recv()
            index = interval * (SUBSTEPS - 1) + sub - 1
            buf = fields[first] if sub == 0 else slabs[index]
            last = sub == SUBSTEPS - 1
            entry = None if sub == 0 and interval == 0 else slab_in[number - 1]
            after = None
            if not last:
                after = slabs[index + 1]
            elif not final:
                after = fields[first + SUBSTEPS]
            acc = zero
            for x in range(width):
                for f in range(tracers):
                    if entry is None:
                        turned = unpack_tile(pack_in[0][f, 0:SLAB, :], x)
                    else:
                        turned = unpack_tile(entry[...], f * width + x)
                    center, value = stencil(buf, f, x, TOP, SLAB, turned)
                    force = jnp.broadcast_to(gate_couple[x : x + 1, :], (SLAB, LANES)) * (
                        jnp.broadcast_to(goal[f, x : x + 1, :], (SLAB, LANES)) - center
                    )
                    sub_row = lax.broadcasted_iota(jnp.int32, (SLAB, LANES), 0)
                    value = value + jnp.where(sub_row == 0, force, 0.0)
                    if after is None:
                        out_ref[f, x, 0:SLAB] = value
                        continue
                    if last:
                        surf[x, f : f + 1] = value[0:1]
                    else:
                        after[f, x + 1, TOP + SLAB : TOP + SLAB + 1] = fields[first + sub + 1][
                            f, x + 1, TOP + SLAB : TOP + SLAB + 1
                        ]
                    after[f, x + 1, TOP : TOP + SLAB] = value
                    after[f, x + 1, TOP - 1 : TOP] = value[0:1]
                    acc = pack_tile(acc, value, f * width + x)
            if after is None:
                return []
            slab_out[number][...] = acc
            return slab_halo(number, after)

        for copy in slab_pending:
            copy.wait_recv()
        slab_pending = []
        bulk_step(0)

        if interval == 0:
            wait_whole(label_in, route_recv.at[INTERVALS])
            heard = label_in[...].reshape(tiles, LANES).astype(jnp.bfloat16)
            slots = tiles * rows
            spread_a = lax.broadcasted_iota(jnp.int32, (LANES, slots), 0)
            spread_b = lax.broadcasted_iota(jnp.int32, (LANES, slots), 1)
            spread = jnp.where(spread_a == spread_b % rows, 1.0, 0.0).astype(jnp.bfloat16)
            table = jnp.dot(heard, spread, preferred_element_type=jnp.float32)
            own_a = lax.broadcasted_iota(jnp.int32, (tiles, slots), 0)
            own_b = lax.broadcasted_iota(jnp.int32, (tiles, slots), 1)
            label_row = jnp.sum(jnp.where(own_a == own_b // rows, table, 0.0), axis=0, keepdims=True)
            block_ids = lax.broadcasted_iota(jnp.int32, (width, slots), 0) + 1
            dense_v[...] = jnp.where(block_ids.astype(jnp.float32) == label_row, 1.0, 0.0).astype(
                jnp.bfloat16
            )
        wait_whole(recvs[interval], route_recv.at[interval])
        dense = dense_v[...]
        for f in range(tracers):
            value = recvs[interval][:, :, f * LANES : (f + 1) * LANES].reshape(tiles * rows, LANES)
            goal[f] = sea * pick(dense, value)

        for sub in range(SUBSTEPS):
            slab_pending = near_step(sub, slab_number, slab_pending)
            if not (sub == SUBSTEPS - 1 and final):
                slab_number += 1
            if sub < SUBSTEPS - 1:
                bulk_step(sub + 1)

    for f in range(tracers):
        out_copy(f, 0, SLAB, 1).start()
    for copy in started:
        copy.wait_send()
    for n in range(count):
        for f in range(tracers):
            for copy in bulk_halo(n, f):
                copy.wait_send()
    for interval in range(INTERVALS):
        wait_whole(sends[interval], route_send.at[interval])
    wait_whole(label_out, route_send.at[INTERVALS])
    for f in range(tracers):
        out_copy(f, SLAB, levels, 0).wait()
        out_copy(f, 0, SLAB, 1).wait()


def body(
    n_gx,
    n_gy,
    state,
    diffusion,
    vertical,
    coupling,
    land_sea,
    route_tile,
    route_src,
    route_dst,
    pair_cols,
    intersection,
):
    _, tracers, levels, width, lanes = state.shape
    assert lanes == LANES and n_gy == 2 and 2 * tracers * width <= LANES and n_gx % 2 == 0
    tiles = n_gx * n_gy
    pairs = route_src.shape[2]
    slots = max(2, 2 * pairs // tiles)
    rows = -(-slots // 8) * 8
    dims = (n_gx, n_gy, tiles, rows, pairs, tracers, levels, width)
    count = INTERVALS * SUBSTEPS
    slab_count = INTERVALS * (SUBSTEPS - 1) + 1
    f32 = jnp.float32
    groups = levels // SLAB
    pack_rows = -(-groups // (LANES // (2 * width))) * SLAB
    halos = count * tracers + slab_count
    scratch = [
        pltpu.VMEM((tracers * levels * width, LANES), f32),
        pltpu.VMEM(intersection.shape[2:], jnp.bfloat16),
        pltpu.VMEM((tracers, width, levels, LANES), f32),
        pltpu.VMEM(diffusion.shape, f32),
        pltpu.VMEM(vertical.shape, f32),
        pltpu.VMEM(coupling.shape, f32),
        pltpu.VMEM(land_sea.shape, jnp.int32),
        pltpu.VMEM(route_src.shape, jnp.int32),
        pltpu.SMEM(route_src.shape, jnp.int32),
        pltpu.VMEM(route_dst.shape, jnp.int32),
        pltpu.SMEM(pair_cols.shape, jnp.int32),
    ]
    scratch += [pltpu.VMEM((tracers, width + 2, TOP + levels + 8, LANES), f32)] * count
    scratch += [pltpu.VMEM((tracers, width + 2, TOP + SLAB + 8, LANES), f32)] * (
        INTERVALS * (SUBSTEPS - 1)
    )
    scratch += [pltpu.VMEM((tracers, pack_rows, LANES), f32)] * (2 * count)
    scratch += [pltpu.VMEM((SLAB, LANES), f32)] * (2 * slab_count)
    scratch += [pltpu.VMEM((tiles, rows, tracers * LANES), f32)] * (2 * INTERVALS)
    scratch += [
        pltpu.VMEM((tiles, 1, LANES), f32),
        pltpu.VMEM((tiles, 1, LANES), f32),
        pltpu.VMEM((width, 8, LANES), f32),
        pltpu.VMEM((pairs * 8, LANES), f32),
        pltpu.VMEM((width, LANES), f32),
        pltpu.VMEM((width, LANES), f32),
        pltpu.VMEM((width, LANES), f32),
        pltpu.VMEM((levels, LANES), f32),
        pltpu.VMEM((tracers, width, LANES), f32),
        pltpu.VMEM((tiles * rows, pairs), jnp.bfloat16),
        pltpu.VMEM((width, tiles * rows), jnp.bfloat16),
        pltpu.SemaphoreType.DMA((10,)),
        pltpu.SemaphoreType.DMA((halos, 3)),
        pltpu.SemaphoreType.DMA((halos, 3)),
        pltpu.SemaphoreType.DMA((INTERVALS + 1,)),
        pltpu.SemaphoreType.DMA((INTERVALS + 1,)),
        pltpu.SemaphoreType.DMA((2 * tracers,)),
    ]
    hbm = pl.BlockSpec(memory_space=pl.ANY)
    out = pl.pallas_call(
        functools.partial(kernel, dims),
        out_shape=jax.ShapeDtypeStruct((tracers, width, levels, LANES), f32),
        in_specs=[hbm] * 10,
        out_specs=hbm,
        scratch_shapes=scratch,
        compiler_params=pltpu.CompilerParams(
            collective_id=0, has_side_effects=True, vmem_limit_bytes=63 * 2**20
        ),
        cost_estimate=pl.CostEstimate(flops=60_000_000, bytes_accessed=5_000_000, transcendentals=0),
        name="coupled_columns",
    )(
        state.reshape(tracers * levels * width, LANES),
        diffusion,
        vertical,
        coupling,
        land_sea,
        route_tile.reshape(route_src.shape),
        route_src,
        route_dst,
        pair_cols,
        intersection.reshape(intersection.shape[2:]),
    )
    return jnp.transpose(out, (0, 2, 1, 3)).reshape(state.shape)


def solution(mesh):
    in_specs = (
        P("comp", None, None, "gx", "gy"),
        P("comp", "gx", "gy"),
        P("comp", None),
        P("comp", "gx", "gy"),
        P("comp", "gx", "gy"),
        P("comp", ("gx", "gy"), None, None),
        P("comp", ("gx", "gy"), None),
        P("comp", ("gx", "gy"), None),
        P("comp", ("gx", "gy"), None),
        P("comp", ("gx", "gy"), None, None, None),
    )
    out_specs = P("comp", None, None, "gx", "gy")
    run = functools.partial(body, mesh.shape["gx"], mesh.shape["gy"])
    return jax.shard_map(run, mesh=mesh, in_specs=in_specs, out_specs=out_specs, check_vma=False)
```
